32 devices in a mesh: band: 4 (over y, x), lon: 8 (over z, core).
Axes of the slice: x: 2, y: 2, z: 4, core: 2. Of those that a mesh axis runs over, the one named last changes fastest.
Arguments:
- sky_maps: float32 [16, 512, 256], P(None, ('band', 'lon')), may hold values from -9 to 9
- noise_var: float32 [512, 256], P(('band', 'lon')), may hold values from 1 to 4
- position: float32 [3, 512, 256], P(None, ('band', 'lon')), may hold values from -1 to 1
- leaf_basis: float32 [512, 256, 64], P(('band', 'lon')), may hold values from -1 to 1
- leaf_couple: float32 [512, 4, 64, 64], P(('band', 'lon')), as said below
- transfer: float32 [512, 64, 64], P(('band', 'lon')), may hold values from -2 to 2
- panel_couple: float32 [64, 2, 64, 64], P(('band', 'lon')), as said below
- near_list: int32 [512, 5], P(('band', 'lon')), may hold values from -1 to 511, as said below
- far_list: int32 [512, 4], P(('band', 'lon')), may hold values from 0 to 511, as said below
- panel_list: int32 [64, 2], P(('band', 'lon')), may hold values from 0 to 63, as said below
- leaf_panel: int32 [512], P(('band', 'lon')), may hold values from 0 to 1
Outputs:
- solution: float32 [16, 512, 256], P(None, ('band', 'lon'))
- residual: float32 [16, 512, 256], P(None, ('band', 'lon'))
The draws below stay inside these ranges and needn't reach their ends.
Inputs may be any that keep to these rules, and one draw needn't show every extreme that they name: `near_list`: entry 0 of a row is the leaf itself; the entries after it that are not -1 come first and are distinct leaves of the same band at cycle distance 1 or 2, the cycle closing; leaf j stands in leaf i's row exactly when i stands in j's. `far_list`: distinct leaves of the same band at cycle distance 3 to 6, the cycle closing; leaf j stands in leaf i's row exactly when i stands in j's. If leaf j stands in slot s of far_list[i] and leaf i in slot t of far_list[j], then leaf_couple[j, t] is the transpose of leaf_couple[i, s]. `panel_list`: entries are panel s of sectors of other bands at the same longitude (sector ids differing by a nonzero multiple of the sectors of a band), s being the panel's own index in its sector; panel j stands in panel k's row as often as k stands in j's. If panel j stands in slot s of panel_list[k] and these slots pair up with the slots t of panel_list[j] that hold k, then panel_couple[j, t] is the transpose of panel_couple[k, s].
All inputs are finite; a program needn't handle non-finite values.
Results may differ from the reference program's by a relative error of at most 0.0003.
Values sent between devices are 32-bit elements; how exact they have to be, the bound alone decides.
A program may use at most 128 MiB of HBM per device.

```python
import math
import jax
import jax.numpy as jnp
from jax import lax

P_SIZE = 256
R = 64
NEAR = 5
FAR1 = 4
FAR2 = 2
REACH = 6
ITERS = 2
PANEL_DEV = 2
LEAF_DEV = 16
MAPS = 16
CYCLE = 128
LEAVES = 512
PANELS = 64


COMMON_PART = 0.5


def corner_mask(rank):
    first_row = jnp.arange(rank)[:, None] == 0
    first_col = jnp.arange(rank)[None, :] == 0
    return jnp.logical_and(first_row, first_col).astype(jnp.float32)


def draw_sky_maps(key, part):
    sector_frac = (jnp.arange(LEAVES) // LEAF_DEV).astype(jnp.float32) / (LEAVES // LEAF_DEV - 1)
    spread = 0.5 * jnp.power(3.0, sector_frac)
    raw_vals = jax.random.truncated_normal(key, -5.0, 5.0, (MAPS, LEAVES, P_SIZE)) + 0.5
    return (raw_vals * spread[None, :, None]).astype(jnp.float32)


def draw_leaf_basis(key, part):
    shape = (LEAVES, P_SIZE, R)
    raw_vals = jax.random.truncated_normal(key, -6.0, 6.0, shape)
    column_shift = jnp.where(jnp.arange(R) == 0, COMMON_PART, 0.0).astype(jnp.float32)
    return ((raw_vals + column_shift[None, None, :]) * P_SIZE ** (-0.5)).astype(jnp.float32)


def draw_transfer(key, part):
    shape = (LEAVES, R, R)
    raw_vals = jax.random.truncated_normal(key, -6.0, 6.0, shape)
    fan_in = R * LEAF_DEV // PANEL_DEV
    return (raw_vals * fan_in ** (-0.5) + COMMON_PART * corner_mask(R)[None]).astype(jnp.float32)


def draw_position(key, part):
    band_count = LEAVES // CYCLE
    leaf_ids = jnp.arange(LEAVES)
    band_of = (leaf_ids // CYCLE).astype(jnp.float32)
    cycle_pos = (leaf_ids % CYCLE).astype(jnp.float32)
    leaf_width = 2.0 * jnp.pi / CYCLE
    center_lat = -1.1 + 2.2 * (band_of + 0.5) / band_count
    center_lon = leaf_width * (cycle_pos + 0.5)
    along_frac = jax.random.uniform(jax.random.fold_in(key, 41), (LEAVES, P_SIZE))
    across_frac = jax.random.uniform(jax.random.fold_in(key, 42), (LEAVES, P_SIZE))
    lon_vals = center_lon[:, None] + leaf_width * (along_frac - 0.5)
    lat_vals = center_lat[:, None] + leaf_width * jnp.cos(center_lat)[:, None] * (across_frac - 0.5)
    return jnp.stack([jnp.cos(lat_vals) * jnp.cos(lon_vals), jnp.cos(lat_vals) * jnp.sin(lon_vals), jnp.sin(lat_vals)], axis=0).astype(jnp.float32)


def draw_near_list(key, part):
    band_count = LEAVES // CYCLE
    leaf_ids = jnp.arange(LEAVES, dtype=jnp.int32)
    band_of = leaf_ids // CYCLE
    cycle_pos = leaf_ids % CYCLE
    polar_band = (jnp.abs(2 * band_of + 1 - band_count) * 2 >= band_count).astype(jnp.int32)
    cutoff = 3 + 6 * polar_band
    edge_one = (jax.random.randint(jax.random.fold_in(key, 31), (LEAVES,), 0, 10) < cutoff).astype(jnp.int32)
    edge_two = (jax.random.randint(jax.random.fold_in(key, 32), (LEAVES,), 0, 10) < cutoff).astype(jnp.int32)
    back_two = band_of * CYCLE + (cycle_pos - 2) % CYCLE
    back_one = band_of * CYCLE + (cycle_pos - 1) % CYCLE
    ahead_one = band_of * CYCLE + (cycle_pos + 1) % CYCLE
    ahead_two = band_of * CYCLE + (cycle_pos + 2) % CYCLE
    cand_ids = jnp.stack([back_two, back_one, ahead_one, ahead_two], axis=1)
    cand_live = jnp.stack([edge_two[back_two], edge_one[back_one], edge_one, edge_two], axis=1)
    leaf_keys = jax.random.split(jax.random.fold_in(key, 33), LEAVES)
    shuffle = jax.vmap(lambda sub_key: jax.random.permutation(sub_key, jnp.arange(4, dtype=jnp.int32)))(leaf_keys)
    cand_ids = jnp.take_along_axis(cand_ids, shuffle, axis=1)
    cand_live = jnp.take_along_axis(cand_live, shuffle, axis=1)
    ranking = jnp.argsort(1 - cand_live, axis=1, stable=True)
    cand_ids = jnp.take_along_axis(cand_ids, ranking, axis=1)
    cand_live = jnp.take_along_axis(cand_live, ranking, axis=1)
    others = jnp.where(cand_live == 1, cand_ids, -1)
    return jnp.concatenate([leaf_ids[:, None], others], axis=1).astype(jnp.int32)


def far_slots(key):
    band_count = LEAVES // CYCLE
    band_of = jnp.arange(LEAVES, dtype=jnp.int32) // CYCLE
    band_keys = jax.random.split(jax.random.fold_in(key, 11), band_count)
    picked = jax.vmap(lambda sub_key: jax.random.permutation(sub_key, jnp.arange(3, REACH + 1, dtype=jnp.int32)))(band_keys)
    picked = picked[:, :FAR1 // 2]
    signed = jnp.concatenate([picked, -picked], axis=1)[band_of]
    leaf_keys = jax.random.split(jax.random.fold_in(key, 12), LEAVES)
    return jax.vmap(lambda sub_key, row_vals: jax.random.permutation(sub_key, row_vals))(leaf_keys, signed)


def far_partners(offsets):
    leaf_ids = jnp.arange(LEAVES, dtype=jnp.int32)
    return (leaf_ids // CYCLE)[:, None] * CYCLE + ((leaf_ids % CYCLE)[:, None] + offsets) % CYCLE


def draw_far_list(key, part):
    return far_partners(far_slots(key)).astype(jnp.int32)


def draw_leaf_couple(key, part):
    offsets = far_slots(key)
    partner = far_partners(offsets)
    leaf_ids = jnp.arange(LEAVES, dtype=jnp.int32)
    shape = (LEAVES, REACH - 2, R, R)
    forward = jax.random.normal(jax.random.fold_in(key, 13), shape)
    forward = forward * (R * FAR1) ** (-0.5)
    source = jnp.where(offsets > 0, leaf_ids[:, None], partner)
    edge_slot = jnp.abs(offsets) - 3
    chosen = forward[source, edge_slot]
    flipped = jnp.swapaxes(chosen, 2, 3)
    return jnp.where((offsets > 0)[:, :, None, None], chosen, flipped).astype(jnp.float32)


def panel_slots(key):
    band_count = LEAVES // CYCLE
    sectors = CYCLE // LEAF_DEV
    panel_ids = jnp.arange(PANELS, dtype=jnp.int32)
    column = panel_ids // PANEL_DEV % sectors
    band_steps = jax.random.randint(jax.random.fold_in(key, 21), (sectors,), 1, band_count // 2 + 1)[column]
    swap_flag = jax.random.randint(jax.random.fold_in(key, 22), (PANELS,), 0, 2)
    first_step = jnp.where(swap_flag == 1, -band_steps, band_steps)
    return jnp.stack([first_step, -first_step], axis=1)


def panel_partners(offsets):
    band_count = LEAVES // CYCLE
    band_panels = PANEL_DEV * (CYCLE // LEAF_DEV)
    panel_ids = jnp.arange(PANELS, dtype=jnp.int32)
    band_of = panel_ids // band_panels
    within = panel_ids % band_panels
    return (band_of[:, None] + offsets) % band_count * band_panels + within[:, None]


def draw_panel_list(key, part):
    return panel_partners(panel_slots(key)).astype(jnp.int32)


def draw_panel_couple(key, part):
    offsets = panel_slots(key)
    partner = panel_partners(offsets)
    panel_ids = jnp.arange(PANELS, dtype=jnp.int32)
    shape = (PANELS, R, R)
    forward = jax.random.normal(jax.random.fold_in(key, 23), shape)
    forward = forward * (R * FAR2) ** (-0.5) + COMMON_PART * corner_mask(R)[None]
    source = jnp.where(offsets > 0, panel_ids[:, None], partner)
    chosen = forward[source]
    flipped = jnp.swapaxes(chosen, 2, 3)
    return jnp.where((offsets > 0)[:, :, None, None], chosen, flipped).astype(jnp.float32)


def plant(entries, stream_key, least, top_value):
    longest = entries.shape.index(max(entries.shape))
    spots = []
    for shift in (0, 1):
        where = [jax.random.randint(jax.random.fold_in(stream_key, axis), (), 0, length) for axis, length in enumerate(entries.shape)]
        where[longest] = (where[longest] + shift) % entries.shape[longest]
        spots.append(tuple(where))
    return entries.at[spots[0]].set(least).at[spots[1]].set(top_value)


def steps_of(own_key, dims, shards, smallest, largest):
    gain = 1.0
    for axis_at, blocks in shards:
        heights = jax.random.uniform(jax.random.fold_in(jax.random.fold_in(own_key, 6), axis_at), (blocks,), jnp.float32, smallest / len(shards), largest / len(shards))
        gain = gain * jnp.repeat(jnp.exp(heights), dims[axis_at] // blocks).reshape((-1,) + (1,) * (len(dims) - 1 - axis_at))
    return gain


def setup_inputs(seed: int = 0) -> dict:
    seeds = jax.random.split(jax.random.key(seed), 12)
    sky_maps = draw_sky_maps(jax.random.fold_in(seeds[11], 71), 0)
    noise_var = jnp.clip(jnp.exp(math.log(4.0) - 1.3862944 * jax.random.uniform(seeds[1], (LEAVES, P_SIZE), jnp.float32) ** steps_of(seeds[1], (LEAVES, P_SIZE), ((0, 32),), -0.2, 0.2)), 1.0, 4.0)
    position = draw_position(jax.random.fold_in(seeds[11], 71), 0)
    leaf_basis = draw_leaf_basis(jax.random.fold_in(seeds[11], 71), 0)
    leaf_couple = draw_leaf_couple(jax.random.fold_in(seeds[11], 71), 0)
    transfer = draw_transfer(jax.random.fold_in(seeds[11], 71), 0)
    panel_couple = draw_panel_couple(jax.random.fold_in(seeds[11], 71), 0)
    near_list = draw_near_list(jax.random.fold_in(seeds[11], 71), 0)
    far_list = draw_far_list(jax.random.fold_in(seeds[11], 71), 0)
    panel_list = draw_panel_list(jax.random.fold_in(seeds[11], 71), 0)
    leaf_panel = plant(jax.random.randint(seeds[10], (LEAVES,), 0, PANEL_DEV), jax.random.fold_in(seeds[10], 1), 0, PANEL_DEV - 1).astype(jnp.int32)
    return {"sky_maps": sky_maps, "noise_var": noise_var, "position": position, "leaf_basis": leaf_basis, "leaf_couple": leaf_couple, "transfer": transfer, "panel_couple": panel_couple, "near_list": near_list, "far_list": far_list, "panel_list": panel_list, "leaf_panel": leaf_panel}


HIGHEST_PRECISION = lax.Precision.HIGHEST
ROOT_THREE = math.sqrt(3.0)
AMPLITUDE = 0.02

def matern_block(rows_pos, cols_pos, length_scale):
    squared = jnp.zeros((cols_pos.shape[1], rows_pos.shape[1], cols_pos.shape[2]), jnp.float32)
    for component in range(3):
        offset = rows_pos[component][None, :, None] - cols_pos[component][:, None, :]
        squared = squared + offset * offset
    scaled = ROOT_THREE * jnp.sqrt(squared) / length_scale
    return AMPLITUDE * (1.0 + scaled) * jnp.exp(-scaled)

def near_field(values, position, near_list, length_scale):
    map_count = values.shape[0]
    slot_valid = near_list >= 0
    safe_ids = jnp.where(slot_valid, near_list, near_list[:, :1]).astype(jnp.int32)
    slot_mask = slot_valid.astype(jnp.float32)
    block_count = LEAVES // LEAF_DEV
    rows_all = jnp.transpose(position, (1, 0, 2)).reshape(block_count, LEAF_DEV, 3, P_SIZE)
    cols_all = jnp.transpose(position[:, safe_ids], (1, 0, 2, 3)).reshape(block_count, LEAF_DEV, 3, NEAR, P_SIZE)
    vals_all = jnp.transpose(values[:, safe_ids], (1, 0, 2, 3)).reshape(block_count, LEAF_DEV, map_count, NEAR, P_SIZE)
    mask_all = slot_mask.reshape(block_count, LEAF_DEV, NEAR)

    def per_leaf(rows_pos, cols_pos, mask_row, vals_row):
        kernel_block = matern_block(rows_pos, cols_pos, length_scale) * mask_row[:, None, None]
        return jnp.einsum('spq,msq->mp', kernel_block, vals_row, precision=HIGHEST_PRECISION)

    def per_group(leaf_group):
        return jax.vmap(per_leaf)(leaf_group[0], leaf_group[1], leaf_group[2], leaf_group[3])
    result = lax.map(per_group, (rows_all, cols_all, mask_all, vals_all))
    return jnp.transpose(result.reshape(LEAVES, map_count, P_SIZE), (1, 0, 2))

def apply_covariance(values, noise_var, position, leaf_basis, leaf_couple, transfer, panel_couple, near_list, far_list, panel_list, home_panel, length_scale):
    near_part = near_field(values, position, near_list, length_scale)
    coeffs = jnp.einsum('lpr,mlp->mlr', leaf_basis, values, precision=HIGHEST_PRECISION)
    leaf_far = jnp.einsum('lsab,mlsb->mla', leaf_couple, coeffs[:, far_list], precision=HIGHEST_PRECISION)
    upward = jnp.einsum('lab,mla->mlb', transfer, coeffs, precision=HIGHEST_PRECISION)
    panel_coeffs = jnp.zeros((values.shape[0], PANELS, R), jnp.float32).at[:, home_panel].add(upward)
    panel_far = jnp.einsum('ksab,mksb->mka', panel_couple, panel_coeffs[:, panel_list], precision=HIGHEST_PRECISION)
    leaf_far = leaf_far + jnp.einsum('lab,mlb->mla', transfer, panel_far[:, home_panel], precision=HIGHEST_PRECISION)
    far_part = jnp.einsum('lpr,mlr->mlp', leaf_basis, leaf_far, precision=HIGHEST_PRECISION)
    return noise_var[None] * values + near_part + far_part

def reference(sky_maps, noise_var, position, leaf_basis, leaf_couple, transfer, panel_couple, near_list, far_list, panel_list, leaf_panel):
    length_scale = 2.0 * math.pi / CYCLE
    home_panel = (jnp.arange(LEAVES, dtype=jnp.int32) // LEAF_DEV * PANEL_DEV + leaf_panel).astype(jnp.int32)

    def covariance_apply(values):
        return apply_covariance(values, noise_var, position, leaf_basis, leaf_couple, transfer, panel_couple, near_list, far_list, panel_list, home_panel, length_scale)
    solution = jnp.zeros_like(sky_maps)
    residual = sky_maps
    direction = sky_maps
    norm_now = lax.optimization_barrier(jnp.sum(residual * residual, axis=(1, 2)))
    for iteration in range(ITERS):
        applied = covariance_apply(direction)
        step_size = norm_now / lax.optimization_barrier(jnp.sum(direction * applied, axis=(1, 2)))
        solution = solution + step_size[:, None, None] * direction
        residual = residual - step_size[:, None, None] * applied
        if iteration + 1 < ITERS:
            norm_next = lax.optimization_barrier(jnp.sum(residual * residual, axis=(1, 2)))
            direction = residual + (norm_next / norm_now)[:, None, None] * direction
            norm_now = norm_next
    return (solution, residual)
```

```python
import functools
import math

import jax
import jax.numpy as jnp
from jax import lax
from jax.experimental import pallas as pl
from jax.experimental.pallas import tpu as pltpu
from jax.sharding import PartitionSpec as P

REACH = 6
DEPTH = 2
AMPLITUDE = 0.02
F32 = jnp.float32
BF16 = jnp.bfloat16
NN = (((1,), (0,)), ((), ()))
NT = (((1,), (1,)), ((), ()))
MESH = pl.DeviceIdType.MESH
GROUP = 4


def halves(x):
    hi = x.astype(BF16)
    lo = (x - hi.astype(F32)).astype(BF16)
    return hi, lo


def dot3(a, bhi, blo, dims):
    n = a.shape[0]
    hi, lo = halves(a)
    both = lax.dot_general(
        jnp.concatenate([hi, lo], axis=0), bhi, dims, preferred_element_type=F32
    )
    rest = lax.dot_general(hi, blo, dims, preferred_element_type=F32)
    return both[:n] + both[n:] + rest


def kernel(
    cycle,
    n_lon,
    n_band,
    pos_ref,
    sky_ref,
    noise_ref,
    basis_ref,
    couple_ref,
    transfer_ref,
    pcouple_ref,
    near_ref,
    far_ref,
    plist_ref,
    home_ref,
    sol_ref,
    res_ref,
    posx,
    posc,
    v0,
    v1,
    w2,
    c0,
    c1,
    pc0,
    pc1,
    pf,
    vs,
    khi,
    klo,
    bhi,
    blo,
    whi,
    wlo,
    thi,
    tlo,
    ghi,
    glo,
    red_lon,
    red_band,
    send_sem,
    recv_sem,
):
    leaves, maps, pixels = sky_ref.shape
    rank = basis_ref.shape[2]
    panels = pcouple_ref.shape[0]
    slots = far_ref.shape[1]
    near_slots = near_ref.shape[1]
    lon = lax.axis_index("lon")
    band = lax.axis_index("band")
    right = lax.rem(lon + 1, n_lon)
    left = lax.rem(lon + n_lon - 1, n_lon)
    first = band * cycle + lon * leaves
    used = [0]

    def push(src, dst, target):
        at = used[0]
        used[0] += 1
        copy = pltpu.make_async_remote_copy(
            src_ref=src,
            dst_ref=dst,
            send_sem=send_sem.at[at],
            recv_sem=recv_sem.at[at],
            device_id=target,
            device_id_type=MESH,
        )
        copy.start()
        return copy

    def rim_push(buf, depth):
        return [
            push(buf.at[pl.ds(leaves, depth)], buf.at[pl.ds(0, depth)], {"lon": right}),
            push(
                buf.at[pl.ds(depth, depth)],
                buf.at[pl.ds(depth + leaves, depth)],
                {"lon": left},
            ),
        ]

    def axis_push(buf, axis, me, count):
        return [
            push(buf.at[me], buf.at[me], {axis: lax.rem(me + k, count)}) for k in range(1, count)
        ]

    def landed(copies):
        for copy in copies:
            copy.wait_recv()

    pending = []

    barrier = pltpu.get_barrier_semaphore()
    for k in range(1, n_lon):
        pl.semaphore_signal(
            barrier, inc=1, device_id={"lon": lax.rem(lon + k, n_lon)}, device_id_type=MESH
        )
    for k in range(1, n_band):
        pl.semaphore_signal(
            barrier, inc=1, device_id={"band": lax.rem(band + k, n_band)}, device_id_type=MESH
        )
    posx[pl.ds(DEPTH, leaves)] = pos_ref[...]
    v0[pl.ds(DEPTH, leaves)] = sky_ref[...]
    pl.semaphore_wait(barrier, n_lon - 1 + n_band - 1)
    pos_copies = rim_push(posx, DEPTH)
    v0_copies = rim_push(v0, DEPTH)
    pending += pos_copies + v0_copies

    def prepare(i):
        bhi[i], blo[i] = halves(basis_ref[i])
        thi[i], tlo[i] = halves(transfer_ref[i])
        for s in range(slots):
            whi[i, s], wlo[i, s] = halves(couple_ref[i, s])

    def upward(i, value, cx, sums):
        c = dot3(value, bhi[i], blo[i], NN)
        cx[REACH + i] = c
        up = dot3(c, thi[i], tlo[i], NN)
        home = home_ref[0, i]
        return [sums[k] + up * jnp.where(home == k, 1.0, 0.0).astype(F32) for k in range(panels)]

    zero_panels = [jnp.zeros((maps, rank), F32) for _ in range(panels)]

    def first_coeffs(g, sums):
        for u in range(GROUP):
            prepare(g * GROUP + u)
        for u in range(GROUP):
            i = g * GROUP + u
            sums = upward(i, sky_ref[i], c0, sums)
        return sums

    sums = lax.fori_loop(0, leaves // GROUP, first_coeffs, zero_panels)
    for k in range(panels):
        pc0[band, k] = sums[k]
    c0_copies = rim_push(c0, REACH)
    pc0_copies = axis_push(pc0, "band", band, n_band)
    pending += c0_copies + pc0_copies
    for k in range(panels):
        for s in range(plist_ref.shape[1]):
            ghi[k, s], glo[k, s] = halves(pcouple_ref[k, s])

    landed(pos_copies + v0_copies)
    scale = math.sqrt(3.0) / (2.0 * math.pi / cycle)

    def columns(j, carry):
        scaled = posx[j] * scale
        posx_scaled = scaled
        posc[j] = jnp.transpose(posx_scaled)
        hi, lo = halves(v0[j])
        vs[j, pl.ds(0, maps)] = hi
        vs[j, pl.ds(maps, maps)] = lo
        return carry

    lax.fori_loop(0, leaves + 2 * DEPTH, columns, 0)

    def near_product(i):
        values = jnp.concatenate([vs[i + d] for d in range(2 * DEPTH + 1)], axis=1)
        both = lax.dot_general(values, khi[i], NN, preferred_element_type=F32)
        rest = lax.dot_general(values[:maps], klo[i], NN, preferred_element_type=F32)
        return both[:maps] + both[maps:] + rest

    chunk = 64

    def first_near(i, carry):
        rows = posx[DEPTH + i] * scale
        me = near_ref[i, 0]
        for d in range(2 * DEPTH + 1):
            offset = d - DEPTH
            if offset == 0:
                weight = jnp.asarray(AMPLITUDE, F32)
            else:
                weight = jnp.asarray(0.0, F32)
                for s in range(1, near_slots):
                    other = near_ref[i, s]
                    gap = other - me
                    hit = (gap == offset) | (gap == offset - cycle) | (gap == offset + cycle)
                    weight = weight + jnp.where((other >= 0) & hit, AMPLITUDE, 0.0).astype(F32)
            for q in range(0, pixels, chunk):
                squared = None
                for component in range(3):
                    gap = (
                        posc[i + d, pl.ds(q, chunk), component : component + 1]
                        - rows[component : component + 1]
                    )
                    squared = gap * gap if squared is None else squared + gap * gap
                t = squared * lax.rsqrt(jnp.maximum(squared, 1e-30))
                block = (weight + weight * t) * jnp.exp(-t)
                hi, lo = halves(block)
                khi[i, pl.ds(d * pixels + q, chunk)] = hi
                klo[i, pl.ds(d * pixels + q, chunk)] = lo
        v1[DEPTH + i] = noise_ref[pl.ds(i, 1)] * sky_ref[i] + near_product(i)
        return carry

    lax.fori_loop(0, leaves, first_near, 0)

    def panel_far(pcx):
        for k in range(panels):
            total = jnp.zeros((maps, rank), F32)
            for s in range(plist_ref.shape[1]):
                other = plist_ref[k, s] // (n_lon * panels)
                total = total + dot3(pcx[other, k], ghi[k, s], glo[k, s], NT)
            pf[k] = total

    def far(i, cx):
        total = dot3(pf[home_ref[0, i]], thi[i], tlo[i], NT)
        for s in range(slots):
            gap = far_ref[i, s] - (first + i)
            gap = jnp.where(gap > REACH, gap - cycle, gap)
            gap = jnp.where(gap < -REACH, gap + cycle, gap)
            row = jnp.clip(i + REACH + gap, 0, leaves + 2 * REACH - 1)
            total = total + dot3(cx[row], whi[i, s], wlo[i, s], NT)
        return dot3(total, bhi[i], blo[i], NT)

    landed(c0_copies + pc0_copies)
    panel_far(pc0)
    zero = jnp.zeros((maps, pixels), F32)

    def first_far(g, carry):
        sums, rr, pw, ww = carry
        out = []
        for u in range(GROUP):
            i = g * GROUP + u
            w = v1[DEPTH + i] + far(i, c0)
            v1[DEPTH + i] = w
            p = sky_ref[i]
            rr, pw, ww = rr + p * p, pw + p * w, ww + w * w
            out.append(w)
        for u in range(GROUP):
            sums = upward(g * GROUP + u, out[u], c1, sums)
        return sums, rr, pw, ww

    sums, rr, pw, ww = lax.fori_loop(
        0, leaves // GROUP, first_far, (zero_panels, zero, zero, zero)
    )
    v1_copies = rim_push(v1, DEPTH)
    for k in range(panels):
        pc1[band, k] = sums[k]
    c1_copies = rim_push(c1, REACH)
    pc1_copies = axis_push(pc1, "band", band, n_band)
    pending += v1_copies + c1_copies + pc1_copies

    lane = lax.broadcasted_iota(jnp.int32, (maps, 128), 1)

    def packed(parts):
        out = jnp.zeros((maps, 128), F32)
        for at, part in enumerate(parts):
            out = jnp.where(lane == at, jnp.sum(part, axis=1, keepdims=True), out)
        return out

    def total_of(buf, count):
        out = buf[0]
        for k in range(1, count):
            out = out + buf[k]
        return out

    red_lon[0, lon] = packed([rr, pw, ww])
    lon_copies = axis_push(red_lon.at[0], "lon", lon, n_lon)
    pending += lon_copies

    def split_value(j, carry):
        hi, lo = halves(v1[j])
        vs[j, pl.ds(0, maps)] = hi
        vs[j, pl.ds(maps, maps)] = lo
        return carry

    def second_near(i, carry):
        w2[i] = noise_ref[pl.ds(i, 1)] * v1[DEPTH + i] + near_product(i)
        return carry

    lax.fori_loop(DEPTH, leaves + DEPTH, split_value, 0)

    def second_near_pair(g, carry):
        second_near(DEPTH + 2 * g, carry)
        second_near(DEPTH + 2 * g + 1, carry)
        return carry

    lax.fori_loop(0, (leaves - 2 * DEPTH) // 2, second_near_pair, 0)
    landed(lon_copies)
    red_band[0, band] = total_of(red_lon.at[0], n_lon)
    band_copies = axis_push(red_band.at[0], "band", band, n_band)
    pending += band_copies
    landed(v1_copies)
    for j in list(range(DEPTH)) + list(range(leaves + DEPTH, leaves + 2 * DEPTH)):
        split_value(j, 0)
    for i in list(range(DEPTH)) + list(range(leaves - DEPTH, leaves)):
        second_near(i, 0)
    landed(c1_copies + pc1_copies)
    panel_far(pc1)

    landed(band_copies)
    first_sums = total_of(red_band.at[0], n_band)
    rr0, pw0, ww0 = first_sums[:, 0:1], first_sums[:, 1:2], first_sums[:, 2:3]
    step0 = rr0 / pw0
    ratio = (rr0 - 2.0 * step0 * pw0 + step0 * step0 * ww0) / rr0

    def second_far(g, carry):
        rr, pw = carry
        for u in range(GROUP):
            i = g * GROUP + u
            w = w2[i] + far(i, c1)
            p, image = sky_ref[i], v1[DEPTH + i]
            residual = p - step0 * image
            direction = residual + ratio * p
            image = (image - step0 * w) + ratio * image
            sol_ref[i] = direction
            res_ref[i] = residual
            w2[i] = image
            rr, pw = rr + residual * residual, pw + direction * image
        return rr, pw

    rr, pw = lax.fori_loop(0, leaves // GROUP, second_far, (zero, zero))
    red_lon[1, lon] = packed([rr, pw])
    lon_copies = axis_push(red_lon.at[1], "lon", lon, n_lon)
    landed(lon_copies)
    red_band[1, band] = total_of(red_lon.at[1], n_lon)
    band_copies = axis_push(red_band.at[1], "band", band, n_band)
    landed(band_copies)
    pending += lon_copies + band_copies
    second_sums = total_of(red_band.at[1], n_band)
    step1 = second_sums[:, 0:1] / second_sums[:, 1:2]

    def finish(i, carry):
        sol_ref[i] = step0 * sky_ref[i] + step1 * sol_ref[i]
        res_ref[i] = res_ref[i] - step1 * w2[i]
        return carry

    lax.fori_loop(0, leaves, finish, 0)
    for copy in pending:
        copy.wait_send()


def on_device(
    sky_maps,
    noise_var,
    position,
    leaf_basis,
    leaf_couple,
    transfer,
    panel_couple,
    near_list,
    far_list,
    panel_list,
    leaf_panel,
):
    n_lon = lax.axis_size("lon")
    n_band = lax.axis_size("band")
    maps, leaves, pixels = sky_maps.shape
    rank = leaf_basis.shape[2]
    panels = panel_couple.shape[0]
    slots = far_list.shape[1]
    pslots = panel_list.shape[1]
    span = 2 * DEPTH + 1
    count = 4 * 2 + 2 * 2 + 4 * (n_band - 1) + 2 * (n_lon - 1)
    vmem = pl.BlockSpec(memory_space=pltpu.VMEM)
    smem = pl.BlockSpec(memory_space=pltpu.SMEM)
    field = jnp.transpose(sky_maps, (1, 0, 2))
    rows = jnp.pad(jnp.transpose(position, (1, 0, 2)), ((0, 0), (0, 5), (0, 0)))
    shape = jax.ShapeDtypeStruct((leaves, maps, pixels), F32)
    sol, res = pl.pallas_call(
        functools.partial(kernel, leaves * n_lon, n_lon, n_band),
        out_shape=(shape, shape),
        in_specs=[vmem] * 7 + [smem] * 4,
        out_specs=(vmem, vmem),
        scratch_shapes=[
            pltpu.VMEM((leaves + 2 * DEPTH, 8, pixels), F32),
            pltpu.VMEM((leaves + 2 * DEPTH, pixels, 8), F32),
            pltpu.VMEM((leaves + 2 * DEPTH, maps, pixels), F32),
            pltpu.VMEM((leaves + 2 * DEPTH, maps, pixels), F32),
            pltpu.VMEM((leaves, maps, pixels), F32),
            pltpu.VMEM((leaves + 2 * REACH, maps, rank), F32),
            pltpu.VMEM((leaves + 2 * REACH, maps, rank), F32),
            pltpu.VMEM((n_band, panels, maps, rank), F32),
            pltpu.VMEM((n_band, panels, maps, rank), F32),
            pltpu.VMEM((panels, maps, rank), F32),
            pltpu.VMEM((leaves + 2 * DEPTH, 2 * maps, pixels), BF16),
            pltpu.VMEM((leaves, span * pixels, pixels), BF16),
            pltpu.VMEM((leaves, span * pixels, pixels), BF16),
            pltpu.VMEM((leaves, pixels, rank), BF16),
            pltpu.VMEM((leaves, pixels, rank), BF16),
            pltpu.VMEM((leaves, slots, rank, rank), BF16),
            pltpu.VMEM((leaves, slots, rank, rank), BF16),
            pltpu.VMEM((leaves, rank, rank), BF16),
            pltpu.VMEM((leaves, rank, rank), BF16),
            pltpu.VMEM((panels, pslots, rank, rank), BF16),
            pltpu.VMEM((panels, pslots, rank, rank), BF16),
            pltpu.VMEM((2, n_lon, maps, 128), F32),
            pltpu.VMEM((2, n_band, maps, 128), F32),
            pltpu.SemaphoreType.DMA((count,)),
            pltpu.SemaphoreType.DMA((count,)),
        ],
        compiler_params=pltpu.CompilerParams(
            collective_id=0, has_side_effects=True, vmem_limit_bytes=56 * 1024 * 1024
        ),
        cost_estimate=pl.CostEstimate(
            flops=4 * leaves * span * pixels * pixels * maps,
            bytes_accessed=8 * 1024 * 1024,
            transcendentals=2 * leaves * span * pixels * pixels,
        ),
    )(
        rows,
        field,
        noise_var,
        leaf_basis,
        leaf_couple,
        transfer,
        panel_couple,
        near_list,
        far_list,
        panel_list,
        leaf_panel[None],
    )
    return (jnp.transpose(sol, (1, 0, 2)), jnp.transpose(res, (1, 0, 2)))


def solution(mesh):
    placed = (
        P(None, ("band", "lon"), None),
        P(("band", "lon"), None),
        P(None, ("band", "lon"), None),
        P(("band", "lon"), None, None),
        P(("band", "lon"), None, None, None),
        P(("band", "lon"), None, None),
        P(("band", "lon"), None, None, None),
        P(("band", "lon"), None),
        P(("band", "lon"), None),
        P(("band", "lon"), None),
        P(("band", "lon")),
    )
    return jax.shard_map(
        on_device,
        mesh=mesh,
        in_specs=placed,
        out_specs=(P(None, ("band", "lon"), None), P(None, ("band", "lon"), None)),
        check_vma=False,
    )
```

```python
import functools
import math

import jax
import jax.numpy as jnp
from jax import lax
from jax.experimental import pallas as pl
from jax.experimental.pallas import tpu as pltpu
from jax.sharding import PartitionSpec as P

REACH = 6
DEPTH = 2
AMPLITUDE = 0.02
F32 = jnp.float32
BF16 = jnp.bfloat16
NN = (((1,), (0,)), ((), ()))
NT = (((1,), (1,)), ((), ()))
MESH = pl.DeviceIdType.MESH
GROUP = 8


def halves(x):
    hi = x.astype(BF16)
    lo = (x - hi.astype(F32)).astype(BF16)
    return hi, lo


def dot3(a, bhi, blo, dims):
    n = a.shape[0]
    hi, lo = halves(a)
    both = lax.dot_general(
        jnp.concatenate([hi, lo], axis=0), bhi, dims, preferred_element_type=F32
    )
    rest = lax.dot_general(hi, blo, dims, preferred_element_type=F32)
    return both[:n] + both[n:] + rest


def kernel(
    cycle,
    n_lon,
    n_band,
    pos_ref,
    sky_ref,
    noise_ref,
    basis_ref,
    couple_ref,
    transfer_ref,
    pcouple_ref,
    near_ref,
    far_ref,
    plist_ref,
    home_ref,
    sol_ref,
    res_ref,
    posx,
    posc,
    v0,
    v1,
    w2,
    dirs,
    resid,
    c0,
    c1,
    pc0,
    pc1,
    pf,
    vs,
    khi,
    klo,
    bhi,
    blo,
    whi,
    wlo,
    thi,
    tlo,
    ghi,
    glo,
    red_lon,
    red_band,
    send_sem,
    recv_sem,
):
    maps, leaves, pixels = sky_ref.shape
    rank = basis_ref.shape[1]
    panels = pcouple_ref.shape[0]
    slots = far_ref.shape[0]
    near_slots = near_ref.shape[0]
    lon = lax.axis_index("lon")
    band = lax.axis_index("band")
    right = lax.rem(lon + 1, n_lon)
    left = lax.rem(lon + n_lon - 1, n_lon)
    first = band * cycle + lon * leaves
    used = [0]

    def push(src, dst, target):
        at = used[0]
        used[0] += 1
        copy = pltpu.make_async_remote_copy(
            src_ref=src,
            dst_ref=dst,
            send_sem=send_sem.at[at],
            recv_sem=recv_sem.at[at],
            device_id=target,
            device_id_type=MESH,
        )
        copy.start()
        return copy

    def rim_push(buf, depth):
        return [
            push(buf.at[pl.ds(leaves, depth)], buf.at[pl.ds(0, depth)], {"lon": right}),
            push(
                buf.at[pl.ds(depth, depth)],
                buf.at[pl.ds(depth + leaves, depth)],
                {"lon": left},
            ),
        ]

    def axis_push(buf, axis, me, count):
        return [
            push(buf.at[me], buf.at[me], {axis: lax.rem(me + k, count)}) for k in range(1, count)
        ]

    def landed(copies):
        for copy in copies:
            copy.wait_recv()

    pending = []

    barrier = pltpu.get_barrier_semaphore()
    for k in range(1, n_lon):
        pl.semaphore_signal(
            barrier, inc=1, device_id={"lon": lax.rem(lon + k, n_lon)}, device_id_type=MESH
        )
    for k in range(1, n_band):
        pl.semaphore_signal(
            barrier, inc=1, device_id={"band": lax.rem(band + k, n_band)}, device_id_type=MESH
        )
    posx[pl.ds(DEPTH, leaves)] = jnp.zeros((leaves,) + posx.shape[1:], F32)
    for i in range(leaves):
        v0[DEPTH + i] = sky_ref[:, i, :]
        for component in range(3):
            posx[DEPTH + i, component : component + 1] = pos_ref[component, i : i + 1]
    pl.semaphore_wait(barrier, n_lon - 1 + n_band - 1)
    pos_copies = rim_push(posx, DEPTH)
    v0_copies = rim_push(v0, DEPTH)
    pending += pos_copies + v0_copies

    def prepare(i):
        bhi[i], blo[i] = halves(basis_ref[i])
        thi[i], tlo[i] = halves(transfer_ref[i])
        for s in range(slots):
            whi[i, s], wlo[i, s] = halves(couple_ref[i, s])

    def upward(g, values, cx, sums):
        ids = [g * GROUP + u for u in range(GROUP)]
        cs = [dot3(values[u], bhi[i], blo[i], NT) for u, i in enumerate(ids)]
        ups = [dot3(cs[u], thi[i], tlo[i], NN) for u, i in enumerate(ids)]
        for u, i in enumerate(ids):
            cx[REACH + i] = cs[u]
            sums = [
                sums[k] + ups[u] * jnp.where(home_ref[0, i] == k, 1.0, 0.0).astype(F32)
                for k in range(panels)
            ]
        return sums

    zero_panels = [jnp.zeros((maps, rank), F32) for _ in range(panels)]

    def first_coeffs(g, sums):
        for u in range(GROUP):
            prepare(g * GROUP + u)
        return upward(g, [v0[DEPTH + g * GROUP + u] for u in range(GROUP)], c0, sums)

    sums = lax.fori_loop(0, leaves // GROUP, first_coeffs, zero_panels)
    for k in range(panels):
        pc0[band, k] = sums[k]
    c0_copies = rim_push(c0, REACH)
    pc0_copies = axis_push(pc0, "band", band, n_band)
    pending += c0_copies + pc0_copies
    for k in range(panels):
        for s in range(plist_ref.shape[1]):
            ghi[k, s], glo[k, s] = halves(pcouple_ref[k, s])

    landed(pos_copies + v0_copies)
    log2e = 1.0 / math.log(2.0)
    scale = log2e * math.sqrt(3.0) / (2.0 * math.pi / cycle)

    def columns(j, carry):
        posc[j] = jnp.transpose(posx[j] * scale)
        hi, lo = halves(v0[j])
        vs[j, pl.ds(0, maps)] = hi
        vs[j, pl.ds(maps, maps)] = lo
        return carry

    lax.fori_loop(0, leaves + 2 * DEPTH, columns, 0)

    def near_product(i):
        values = jnp.concatenate([vs[i + d] for d in range(2 * DEPTH + 1)], axis=1)
        both = lax.dot_general(values, khi[i], NN, preferred_element_type=F32)
        rest = lax.dot_general(values[:maps], klo[i], NN, preferred_element_type=F32)
        return both[:maps] + both[maps:] + rest

    chunk = 64

    def first_near(i, carry):
        rows = posx[DEPTH + i] * scale
        me = near_ref[0, i]
        total = noise_ref[pl.ds(i, 1)] * v0[DEPTH + i]
        for d in range(2 * DEPTH + 1):
            offset = d - DEPTH
            if offset == 0:
                weight = jnp.asarray(AMPLITUDE, F32)
            else:
                weight = jnp.asarray(0.0, F32)
                for s in range(1, near_slots):
                    other = near_ref[s, i]
                    gap = other - me
                    hit = (gap == offset) | (gap == offset - cycle) | (gap == offset + cycle)
                    weight = weight + jnp.where((other >= 0) & hit, AMPLITUDE, 0.0).astype(F32)
            slope = weight * math.log(2.0)
            for q in range(0, pixels, chunk):
                squared = None
                for component in range(3):
                    gap = (
                        posc[i + d, pl.ds(q, chunk), component : component + 1]
                        - rows[component : component + 1]
                    )
                    squared = gap * gap if squared is None else squared + gap * gap
                t = squared * lax.rsqrt(jnp.maximum(squared, 1e-30))
                block = (weight + slope * t) * jnp.exp2(-t)
                hi, lo = halves(block)
                khi[i, pl.ds(d * pixels + q, chunk)] = hi
                klo[i, pl.ds(d * pixels + q, chunk)] = lo
            values = vs[i + d]
            at = pl.ds(d * pixels, pixels)
            both = lax.dot_general(values, khi[i, at], NN, preferred_element_type=F32)
            rest = lax.dot_general(values[:maps], klo[i, at], NN, preferred_element_type=F32)
            total = total + (both[:maps] + both[maps:] + rest)
        v1[DEPTH + i] = total
        return carry

    lax.fori_loop(0, leaves, first_near, 0)

    def panel_far(pcx):
        for k in range(panels):
            total = jnp.zeros((maps, rank), F32)
            for s in range(plist_ref.shape[1]):
                other = plist_ref[k, s] // (n_lon * panels)
                total = total + dot3(pcx[other, k], ghi[k, s], glo[k, s], NT)
            pf[k] = total

    def far(i, cx):
        total = dot3(pf[home_ref[0, i]], thi[i], tlo[i], NT)
        for s in range(slots):
            gap = far_ref[s, i] - (first + i)
            gap = jnp.where(gap > REACH, gap - cycle, gap)
            gap = jnp.where(gap < -REACH, gap + cycle, gap)
            row = jnp.clip(i + REACH + gap, 0, leaves + 2 * REACH - 1)
            total = total + dot3(cx[row], whi[i, s], wlo[i, s], NT)
        return dot3(total, bhi[i], blo[i], NN)

    landed(c0_copies + pc0_copies)
    panel_far(pc0)
    zero = jnp.zeros((maps, pixels), F32)

    def first_far(g, carry):
        sums, rr, pw, ww = carry
        fars = [far(g * GROUP + u, c0) for u in range(GROUP)]
        out = [v1[DEPTH + g * GROUP + u] + fars[u] for u in range(GROUP)]
        sums = upward(g, out, c1, sums)
        for u in range(GROUP):
            i = g * GROUP + u
            p, w = v0[DEPTH + i], out[u]
            v1[DEPTH + i] = w
            rr, pw, ww = rr + p * p, pw + p * w, ww + w * w
        return sums, rr, pw, ww

    sums, rr, pw, ww = lax.fori_loop(
        0, leaves // GROUP, first_far, (zero_panels, zero, zero, zero)
    )
    v1_copies = rim_push(v1, DEPTH)
    for k in range(panels):
        pc1[band, k] = sums[k]
    c1_copies = rim_push(c1, REACH)
    pc1_copies = axis_push(pc1, "band", band, n_band)
    pending += v1_copies + c1_copies + pc1_copies

    lane = lax.broadcasted_iota(jnp.int32, (maps, 128), 1)

    def packed(parts):
        out = jnp.zeros((maps, 128), F32)
        for at, part in enumerate(parts):
            out = jnp.where(lane == at, jnp.sum(part, axis=1, keepdims=True), out)
        return out

    def total_of(buf, count):
        out = buf[0]
        for k in range(1, count):
            out = out + buf[k]
        return out

    red_lon[0, lon] = packed([rr, pw, ww])
    lon_copies = axis_push(red_lon.at[0], "lon", lon, n_lon)
    pending += lon_copies

    def split_value(j, carry):
        hi, lo = halves(v1[j])
        vs[j, pl.ds(0, maps)] = hi
        vs[j, pl.ds(maps, maps)] = lo
        return carry

    def second_near(i, carry):
        w2[i] = noise_ref[pl.ds(i, 1)] * v1[DEPTH + i] + near_product(i)
        return carry

    lax.fori_loop(DEPTH, leaves + DEPTH, split_value, 0)

    batch = 2 * DEPTH

    def second_near_batch(g, carry):
        for u in range(batch):
            second_near(DEPTH + batch * g + u, carry)
        return carry

    lax.fori_loop(0, (leaves - 2 * DEPTH) // batch, second_near_batch, 0)
    landed(lon_copies)
    red_band[0, band] = total_of(red_lon.at[0], n_lon)
    band_copies = axis_push(red_band.at[0], "band", band, n_band)
    pending += band_copies
    landed(v1_copies)
    for j in list(range(DEPTH)) + list(range(leaves + DEPTH, leaves + 2 * DEPTH)):
        split_value(j, 0)
    for i in list(range(DEPTH)) + list(range(leaves - DEPTH, leaves)):
        second_near(i, 0)
    landed(c1_copies + pc1_copies)
    panel_far(pc1)

    landed(band_copies)
    first_sums = total_of(red_band.at[0], n_band)
    rr0, pw0, ww0 = first_sums[:, 0:1], first_sums[:, 1:2], first_sums[:, 2:3]
    step0 = rr0 / pw0
    ratio = (rr0 - 2.0 * step0 * pw0 + step0 * step0 * ww0) / rr0

    def second_far(g, carry):
        rr, pw = carry
        fars = [far(g * GROUP + u, c1) for u in range(GROUP)]
        for u in range(GROUP):
            i = g * GROUP + u
            w = w2[i] + fars[u]
            p, image = v0[DEPTH + i], v1[DEPTH + i]
            residual = p - step0 * image
            direction = residual + ratio * p
            image = (image - step0 * w) + ratio * image
            dirs[i] = direction
            resid[i] = residual
            w2[i] = image
            rr, pw = rr + residual * residual, pw + direction * image
        return rr, pw

    rr, pw = lax.fori_loop(0, leaves // GROUP, second_far, (zero, zero))
    red_lon[1, lon] = packed([rr, pw])
    lon_copies = axis_push(red_lon.at[1], "lon", lon, n_lon)
    landed(lon_copies)
    red_band[1, band] = total_of(red_lon.at[1], n_lon)
    band_copies = axis_push(red_band.at[1], "band", band, n_band)
    landed(band_copies)
    pending += lon_copies + band_copies
    second_sums = total_of(red_band.at[1], n_band)
    step1 = second_sums[:, 0:1] / second_sums[:, 1:2]

    for i in range(leaves):
        sol_ref[:, i, :] = step0 * v0[DEPTH + i] + step1 * dirs[i]
        res_ref[:, i, :] = resid[i] - step1 * w2[i]
    for copy in pending:
        copy.wait_send()


def on_device(
    sky_maps,
    noise_var,
    position,
    leaf_basis,
    leaf_couple,
    transfer,
    panel_couple,
    near_list,
    far_list,
    panel_list,
    leaf_panel,
):
    n_lon = lax.axis_size("lon")
    n_band = lax.axis_size("band")
    maps, leaves, pixels = sky_maps.shape
    rank = leaf_basis.shape[2]
    panels = panel_couple.shape[0]
    slots = far_list.shape[1]
    pslots = panel_list.shape[1]
    span = 2 * DEPTH + 1
    count = 4 * 2 + 2 * 2 + 4 * (n_band - 1) + 2 * (n_lon - 1)
    vmem = pl.BlockSpec(memory_space=pltpu.VMEM)
    smem = pl.BlockSpec(memory_space=pltpu.SMEM)
    shape = jax.ShapeDtypeStruct((maps, leaves, pixels), F32)
    sol, res = pl.pallas_call(
        functools.partial(kernel, leaves * n_lon, n_lon, n_band),
        out_shape=(shape, shape),
        in_specs=[vmem] * 7 + [smem] * 4,
        out_specs=(vmem, vmem),
        scratch_shapes=[
            pltpu.VMEM((leaves + 2 * DEPTH, 8, pixels), F32),
            pltpu.VMEM((leaves + 2 * DEPTH, pixels, 8), F32),
            pltpu.VMEM((leaves + 2 * DEPTH, maps, pixels), F32),
            pltpu.VMEM((leaves + 2 * DEPTH, maps, pixels), F32),
            pltpu.VMEM((leaves, maps, pixels), F32),
            pltpu.VMEM((leaves, maps, pixels), F32),
            pltpu.VMEM((leaves, maps, pixels), F32),
            pltpu.VMEM((leaves + 2 * REACH, maps, rank), F32),
            pltpu.VMEM((leaves + 2 * REACH, maps, rank), F32),
            pltpu.VMEM((n_band, panels, maps, rank), F32),
            pltpu.VMEM((n_band, panels, maps, rank), F32),
            pltpu.VMEM((panels, maps, rank), F32),
            pltpu.VMEM((leaves + 2 * DEPTH, 2 * maps, pixels), BF16),
            pltpu.VMEM((leaves, span * pixels, pixels), BF16),
            pltpu.VMEM((leaves, span * pixels, pixels), BF16),
            pltpu.VMEM((leaves, rank, pixels), BF16),
            pltpu.VMEM((leaves, rank, pixels), BF16),
            pltpu.VMEM((leaves, slots, rank, rank), BF16),
            pltpu.VMEM((leaves, slots, rank, rank), BF16),
            pltpu.VMEM((leaves, rank, rank), BF16),
            pltpu.VMEM((leaves, rank, rank), BF16),
            pltpu.VMEM((panels, pslots, rank, rank), BF16),
            pltpu.VMEM((panels, pslots, rank, rank), BF16),
            pltpu.VMEM((2, n_lon, maps, 128), F32),
            pltpu.VMEM((2, n_band, maps, 128), F32),
            pltpu.SemaphoreType.DMA((count,)),
            pltpu.SemaphoreType.DMA((count,)),
        ],
        compiler_params=pltpu.CompilerParams(
            collective_id=0, has_side_effects=True, vmem_limit_bytes=56 * 1024 * 1024
        ),
        cost_estimate=pl.CostEstimate(
            flops=4 * leaves * span * pixels * pixels * maps,
            bytes_accessed=8 * 1024 * 1024,
            transcendentals=2 * leaves * span * pixels * pixels,
        ),
    )(
        position,
        sky_maps,
        noise_var,
        jnp.swapaxes(leaf_basis, 1, 2),
        leaf_couple,
        transfer,
        panel_couple,
        near_list.T,
        far_list.T,
        panel_list,
        leaf_panel[None],
    )
    return (sol, res)


def solution(mesh):
    placed = (
        P(None, ("band", "lon"), None),
        P(("band", "lon"), None),
        P(None, ("band", "lon"), None),
        P(("band", "lon"), None, None),
        P(("band", "lon"), None, None, None),
        P(("band", "lon"), None, None),
        P(("band", "lon"), None, None, None),
        P(("band", "lon"), None),
        P(("band", "lon"), None),
        P(("band", "lon"), None),
        P(("band", "lon")),
    )
    return jax.shard_map(
        on_device,
        mesh=mesh,
        in_specs=placed,
        out_specs=(P(None, ("band", "lon"), None), P(None, ("band", "lon"), None)),
        check_vma=False,
    )
```

```python
import functools
import math

import jax
import jax.numpy as jnp
from jax import lax
from jax.experimental import pallas as pl
from jax.experimental.pallas import tpu as pltpu
from jax.sharding import PartitionSpec as P

REACH = 6
DEPTH = 2
AMPLITUDE = 0.02
F32 = jnp.float32
BF16 = jnp.bfloat16
NN = (((1,), (0,)), ((), ()))
NT = (((1,), (1,)), ((), ()))
MESH = pl.DeviceIdType.MESH
GROUP = 8


def halves(x):
    hi = x.astype(BF16)
    lo = (x - hi.astype(F32)).astype(BF16)
    return hi, lo


def dot3(a, bhi, blo, dims):
    n = a.shape[0]
    hi, lo = halves(a)
    both = lax.dot_general(
        jnp.concatenate([hi, lo], axis=0), bhi, dims, preferred_element_type=F32
    )
    rest = lax.dot_general(hi, blo, dims, preferred_element_type=F32)
    return both[:n] + both[n:] + rest


def spread(a, bcat):
    hi, lo = halves(a)
    return lax.dot_general(
        jnp.concatenate([hi, lo], axis=0), bcat, NT, preferred_element_type=F32
    )


def gathered(r):
    n, k = r.shape[0] // 2, r.shape[1] // 2
    return r[:n, :k] + r[n:, :k] + r[:n, k:]


def kernel(
    cycle,
    n_lon,
    n_band,
    pos_ref,
    sky_ref,
    noise_ref,
    basis_ref,
    couple_ref,
    transfer_ref,
    pcouple_ref,
    near_ref,
    far_ref,
    plist_ref,
    home_ref,
    sol_ref,
    res_ref,
    posx,
    posa,
    posb,
    v0,
    v1,
    w2,
    dirs,
    resid,
    c0,
    c1,
    pc0,
    pc1,
    pf,
    vs,
    khi,
    klo,
    bcat,
    wcat,
    tcat,
    ghi,
    glo,
    red_lon,
    red_band,
    send_sem,
    recv_sem,
):
    maps, leaves, pixels = sky_ref.shape
    rank = basis_ref.shape[1]
    panels = pcouple_ref.shape[0]
    slots = far_ref.shape[0]
    near_slots = near_ref.shape[0]
    lon = lax.axis_index("lon")
    band = lax.axis_index("band")
    right = lax.rem(lon + 1, n_lon)
    left = lax.rem(lon + n_lon - 1, n_lon)
    first = band * cycle + lon * leaves
    used = [0]

    def push(src, dst, target):
        at = used[0]
        used[0] += 1
        copy = pltpu.make_async_remote_copy(
            src_ref=src,
            dst_ref=dst,
            send_sem=send_sem.at[at],
            recv_sem=recv_sem.at[at],
            device_id=target,
            device_id_type=MESH,
        )
        copy.start()
        return copy

    def rim_push(buf, depth):
        return [
            push(buf.at[pl.ds(leaves, depth)], buf.at[pl.ds(0, depth)], {"lon": right}),
            push(
                buf.at[pl.ds(depth, depth)],
                buf.at[pl.ds(depth + leaves, depth)],
                {"lon": left},
            ),
        ]

    def axis_push(buf, axis, me, count):
        return [
            push(buf.at[me], buf.at[me], {axis: lax.rem(me + k, count)}) for k in range(1, count)
        ]

    def landed(copies):
        for copy in copies:
            copy.wait_recv()

    pending = []

    barrier = pltpu.get_barrier_semaphore()
    for k in range(1, n_lon):
        pl.semaphore_signal(
            barrier, inc=1, device_id={"lon": lax.rem(lon + k, n_lon)}, device_id_type=MESH
        )
    for k in range(1, n_band):
        pl.semaphore_signal(
            barrier, inc=1, device_id={"band": lax.rem(band + k, n_band)}, device_id_type=MESH
        )
    posx[pl.ds(DEPTH, leaves)] = jnp.zeros((leaves,) + posx.shape[1:], F32)
    for i in range(leaves):
        v0[DEPTH + i] = sky_ref[:, i, :]
        for component in range(3):
            posx[DEPTH + i, component : component + 1] = pos_ref[component, i : i + 1]
    pl.semaphore_wait(barrier, n_lon - 1 + n_band - 1)
    pos_copies = rim_push(posx, DEPTH)
    v0_copies = rim_push(v0, DEPTH)
    pending += pos_copies + v0_copies

    def prepare(i):
        top, low = pl.ds(0, rank), pl.ds(rank, rank)
        bcat[i, top], bcat[i, low] = halves(basis_ref[i])
        tcat[i, top], tcat[i, low] = halves(transfer_ref[i])
        for s in range(slots):
            wcat[i, s, top], wcat[i, s, low] = halves(couple_ref[i, s])

    def upward(g, values, cx, sums):
        ids = [g * GROUP + u for u in range(GROUP)]
        cs = [gathered(spread(values[u], bcat[i])) for u, i in enumerate(ids)]
        ups = [
            dot3(cs[u], tcat[i, pl.ds(0, rank)], tcat[i, pl.ds(rank, rank)], NN)
            for u, i in enumerate(ids)
        ]
        for u, i in enumerate(ids):
            cx[REACH + i] = cs[u]
            sums = [
                sums[k] + ups[u] * jnp.where(home_ref[0, i] == k, 1.0, 0.0).astype(F32)
                for k in range(panels)
            ]
        return sums

    zero_panels = [jnp.zeros((maps, rank), F32) for _ in range(panels)]

    def first_coeffs(g, sums):
        for u in range(GROUP):
            prepare(g * GROUP + u)
        return upward(g, [v0[DEPTH + g * GROUP + u] for u in range(GROUP)], c0, sums)

    sums = lax.fori_loop(0, leaves // GROUP, first_coeffs, zero_panels)
    for k in range(panels):
        pc0[band, k] = sums[k]
    c0_copies = rim_push(c0, REACH)
    pc0_copies = axis_push(pc0, "band", band, n_band)
    pending += c0_copies + pc0_copies
    for k in range(panels):
        for s in range(plist_ref.shape[1]):
            ghi[k, s], glo[k, s] = halves(pcouple_ref[k, s])

    landed(pos_copies + v0_copies)
    log2e = 1.0 / math.log(2.0)
    scale = log2e * math.sqrt(3.0) / (2.0 * math.pi / cycle)

    middle = posx[DEPTH + leaves // 2, :, 0:1]
    ones = jnp.ones((1, pixels), F32)
    spare = jnp.zeros((8, pixels), F32)

    def thirds(x):
        one = x.astype(BF16).astype(F32)
        two = (x - one).astype(BF16).astype(F32)
        return one, two, (x - one) - two

    def columns(j, carry):
        place = ((posx[j] - middle) * scale)[:3]
        one, two, three = thirds(place)
        norms = thirds(jnp.sum(place * place, axis=0, keepdims=True))
        target = [one, one, two, one, three, two]
        source = [one, two, one, three, one, two]
        posa[j] = jnp.concatenate(
            target + list(norms) + [ones] * 3 + [spare], axis=0
        ).astype(BF16)
        source = [-2.0 * x for x in source]
        posb[j] = jnp.transpose(
            jnp.concatenate(source + [ones] * 3 + list(norms) + [spare], axis=0)
        ).astype(BF16)
        hi, lo = halves(v0[j])
        vs[j, pl.ds(0, maps)] = hi
        vs[j, pl.ds(maps, maps)] = lo
        return carry

    lax.fori_loop(0, leaves + 2 * DEPTH, columns, 0)

    def near_product(i):
        values = jnp.concatenate([vs[i + d] for d in range(2 * DEPTH + 1)], axis=1)
        both = lax.dot_general(values, khi[i], NN, preferred_element_type=F32)
        rest = lax.dot_general(values[:maps], klo[i], NN, preferred_element_type=F32)
        return both[:maps] + both[maps:] + rest

    chunk = 128

    def first_near(i, carry):
        rows = posa[DEPTH + i]
        me = near_ref[0, i]
        total = noise_ref[pl.ds(i, 1)] * v0[DEPTH + i]
        for d in range(2 * DEPTH + 1):
            offset = d - DEPTH
            if offset == 0:
                weight = jnp.asarray(AMPLITUDE, F32)
            else:
                weight = jnp.asarray(0.0, F32)
                for s in range(1, near_slots):
                    other = near_ref[s, i]
                    gap = other - me
                    hit = (gap == offset) | (gap == offset - cycle) | (gap == offset + cycle)
                    weight = weight + jnp.where((other >= 0) & hit, AMPLITUDE, 0.0).astype(F32)
            slope = weight * math.log(2.0)
            for q in range(0, pixels, chunk):
                squared = lax.dot_general(
                    posb[i + d, pl.ds(q, chunk)], rows, NN, preferred_element_type=F32
                )
                squared = jnp.maximum(squared, 1e-30)
                t = squared * lax.rsqrt(squared)
                block = (weight + slope * t) * jnp.exp2(-t)
                hi, lo = halves(block)
                khi[i, pl.ds(d * pixels + q, chunk)] = hi
                klo[i, pl.ds(d * pixels + q, chunk)] = lo
            values = vs[i + d]
            at = pl.ds(d * pixels, pixels)
            both = lax.dot_general(values, khi[i, at], NN, preferred_element_type=F32)
            rest = lax.dot_general(values[:maps], klo[i, at], NN, preferred_element_type=F32)
            total = total + (both[:maps] + both[maps:] + rest)
        v1[DEPTH + i] = total
        return carry

    lax.fori_loop(0, leaves, first_near, 0)

    def panel_far(pcx):
        for k in range(panels):
            total = jnp.zeros((maps, rank), F32)
            for s in range(plist_ref.shape[1]):
                other = plist_ref[k, s] // (n_lon * panels)
                total = total + dot3(pcx[other, k], ghi[k, s], glo[k, s], NT)
            pf[k] = total

    def far(i, cx):
        total = spread(pf[home_ref[0, i]], tcat[i])
        for s in range(slots):
            gap = far_ref[s, i] - (first + i)
            gap = jnp.where(gap > REACH, gap - cycle, gap)
            gap = jnp.where(gap < -REACH, gap + cycle, gap)
            row = jnp.clip(i + REACH + gap, 0, leaves + 2 * REACH - 1)
            total = total + spread(cx[row], wcat[i, s])
        return dot3(
            gathered(total), bcat[i, pl.ds(0, rank)], bcat[i, pl.ds(rank, rank)], NN
        )

    landed(c0_copies + pc0_copies)
    panel_far(pc0)
    zero = jnp.zeros((maps, pixels), F32)

    def first_far(g, carry):
        sums, rr, pw, ww = carry
        fars = [far(g * GROUP + u, c0) for u in range(GROUP)]
        out = [v1[DEPTH + g * GROUP + u] + fars[u] for u in range(GROUP)]
        sums = upward(g, out, c1, sums)
        for u in range(GROUP):
            i = g * GROUP + u
            p, w = v0[DEPTH + i], out[u]
            v1[DEPTH + i] = w
            rr, pw, ww = rr + p * p, pw + p * w, ww + w * w
        return sums, rr, pw, ww

    sums, rr, pw, ww = lax.fori_loop(
        0, leaves // GROUP, first_far, (zero_panels, zero, zero, zero)
    )
    v1_copies = rim_push(v1, DEPTH)
    for k in range(panels):
        pc1[band, k] = sums[k]
    c1_copies = rim_push(c1, REACH)
    pc1_copies = axis_push(pc1, "band", band, n_band)
    pending += v1_copies + c1_copies + pc1_copies

    lane = lax.broadcasted_iota(jnp.int32, (maps, 128), 1)

    def packed(parts):
        out = jnp.zeros((maps, 128), F32)
        for at, part in enumerate(parts):
            out = jnp.where(lane == at, jnp.sum(part, axis=1, keepdims=True), out)
        return out

    def total_of(buf, count):
        out = buf[0]
        for k in range(1, count):
            out = out + buf[k]
        return out

    red_lon[0, lon] = packed([rr, pw, ww])
    lon_copies = axis_push(red_lon.at[0], "lon", lon, n_lon)
    pending += lon_copies

    def split_value(j, carry):
        hi, lo = halves(v1[j])
        vs[j, pl.ds(0, maps)] = hi
        vs[j, pl.ds(maps, maps)] = lo
        return carry

    def second_near(i, carry):
        w2[i] = noise_ref[pl.ds(i, 1)] * v1[DEPTH + i] + near_product(i)
        return carry

    lax.fori_loop(DEPTH, leaves + DEPTH, split_value, 0)

    batch = 2 * DEPTH

    def second_near_batch(g, carry):
        for u in range(batch):
            second_near(DEPTH + batch * g + u, carry)
        return carry

    lax.fori_loop(0, (leaves - 2 * DEPTH) // batch, second_near_batch, 0)
    landed(lon_copies)
    red_band[0, band] = total_of(red_lon.at[0], n_lon)
    band_copies = axis_push(red_band.at[0], "band", band, n_band)
    pending += band_copies
    landed(v1_copies)
    for j in list(range(DEPTH)) + list(range(leaves + DEPTH, leaves + 2 * DEPTH)):
        split_value(j, 0)
    for i in list(range(DEPTH)) + list(range(leaves - DEPTH, leaves)):
        second_near(i, 0)
    landed(c1_copies + pc1_copies)
    panel_far(pc1)

    landed(band_copies)
    first_sums = total_of(red_band.at[0], n_band)
    rr0, pw0, ww0 = first_sums[:, 0:1], first_sums[:, 1:2], first_sums[:, 2:3]
    step0 = rr0 / pw0
    ratio = (rr0 - 2.0 * step0 * pw0 + step0 * step0 * ww0) / rr0

    def second_far(g, carry):
        rr, pw = carry
        fars = [far(g * GROUP + u, c1) for u in range(GROUP)]
        for u in range(GROUP):
            i = g * GROUP + u
            w = w2[i] + fars[u]
            p, image = v0[DEPTH + i], v1[DEPTH + i]
            residual = p - step0 * image
            direction = residual + ratio * p
            image = (image - step0 * w) + ratio * image
            dirs[i] = direction
            resid[i] = residual
            w2[i] = image
            rr, pw = rr + residual * residual, pw + direction * image
        return rr, pw

    rr, pw = lax.fori_loop(0, leaves // GROUP, second_far, (zero, zero))
    red_lon[1, lon] = packed([rr, pw])
    lon_copies = axis_push(red_lon.at[1], "lon", lon, n_lon)
    landed(lon_copies)
    red_band[1, band] = total_of(red_lon.at[1], n_lon)
    band_copies = axis_push(red_band.at[1], "band", band, n_band)
    landed(band_copies)
    pending += lon_copies + band_copies
    second_sums = total_of(red_band.at[1], n_band)
    step1 = second_sums[:, 0:1] / second_sums[:, 1:2]

    for i in range(leaves):
        sol_ref[:, i, :] = step0 * v0[DEPTH + i] + step1 * dirs[i]
        res_ref[:, i, :] = resid[i] - step1 * w2[i]
    for copy in pending:
        copy.wait_send()


def on_device(
    sky_maps,
    noise_var,
    position,
    leaf_basis,
    leaf_couple,
    transfer,
    panel_couple,
    near_list,
    far_list,
    panel_list,
    leaf_panel,
):
    n_lon = lax.axis_size("lon")
    n_band = lax.axis_size("band")
    maps, leaves, pixels = sky_maps.shape
    rank = leaf_basis.shape[2]
    panels = panel_couple.shape[0]
    slots = far_list.shape[1]
    pslots = panel_list.shape[1]
    span = 2 * DEPTH + 1
    count = 4 * 2 + 2 * 2 + 4 * (n_band - 1) + 2 * (n_lon - 1)
    vmem = pl.BlockSpec(memory_space=pltpu.VMEM)
    smem = pl.BlockSpec(memory_space=pltpu.SMEM)
    shape = jax.ShapeDtypeStruct((maps, leaves, pixels), F32)
    sol, res = pl.pallas_call(
        functools.partial(kernel, leaves * n_lon, n_lon, n_band),
        out_shape=(shape, shape),
        in_specs=[vmem] * 7 + [smem] * 4,
        out_specs=(vmem, vmem),
        scratch_shapes=[
            pltpu.VMEM((leaves + 2 * DEPTH, 8, pixels), F32),
            pltpu.VMEM((leaves + 2 * DEPTH, 32, pixels), BF16),
            pltpu.VMEM((leaves + 2 * DEPTH, pixels, 32), BF16),
            pltpu.VMEM((leaves + 2 * DEPTH, maps, pixels), F32),
            pltpu.VMEM((leaves + 2 * DEPTH, maps, pixels), F32),
            pltpu.VMEM((leaves, maps, pixels), F32),
            pltpu.VMEM((leaves, maps, pixels), F32),
            pltpu.VMEM((leaves, maps, pixels), F32),
            pltpu.VMEM((leaves + 2 * REACH, maps, rank), F32),
            pltpu.VMEM((leaves + 2 * REACH, maps, rank), F32),
            pltpu.VMEM((n_band, panels, maps, rank), F32),
            pltpu.VMEM((n_band, panels, maps, rank), F32),
            pltpu.VMEM((panels, maps, rank), F32),
            pltpu.VMEM((leaves + 2 * DEPTH, 2 * maps, pixels), BF16),
            pltpu.VMEM((leaves, span * pixels, pixels), BF16),
            pltpu.VMEM((leaves, span * pixels, pixels), BF16),
            pltpu.VMEM((leaves, 2 * rank, pixels), BF16),
            pltpu.VMEM((leaves, slots, 2 * rank, rank), BF16),
            pltpu.VMEM((leaves, 2 * rank, rank), BF16),
            pltpu.VMEM((panels, pslots, rank, rank), BF16),
            pltpu.VMEM((panels, pslots, rank, rank), BF16),
            pltpu.VMEM((2, n_lon, maps, 128), F32),
            pltpu.VMEM((2, n_band, maps, 128), F32),
            pltpu.SemaphoreType.DMA((count,)),
            pltpu.SemaphoreType.DMA((count,)),
        ],
        compiler_params=pltpu.CompilerParams(
            collective_id=0, has_side_effects=True, vmem_limit_bytes=56 * 1024 * 1024
        ),
        cost_estimate=pl.CostEstimate(
            flops=4 * leaves * span * pixels * pixels * maps,
            bytes_accessed=8 * 1024 * 1024,
            transcendentals=2 * leaves * span * pixels * pixels,
        ),
    )(
        position,
        sky_maps,
        noise_var,
        jnp.swapaxes(leaf_basis, 1, 2),
        leaf_couple,
        transfer,
        panel_couple,
        near_list.T,
        far_list.T,
        panel_list,
        leaf_panel[None],
    )
    return (sol, res)


def solution(mesh):
    placed = (
        P(None, ("band", "lon"), None),
        P(("band", "lon"), None),
        P(None, ("band", "lon"), None),
        P(("band", "lon"), None, None),
        P(("band", "lon"), None, None, None),
        P(("band", "lon"), None, None),
        P(("band", "lon"), None, None, None),
        P(("band", "lon"), None),
        P(("band", "lon"), None),
        P(("band", "lon"), None),
        P(("band", "lon")),
    )
    return jax.shard_map(
        on_device,
        mesh=mesh,
        in_specs=placed,
        out_specs=(P(None, ("band", "lon"), None), P(None, ("band", "lon"), None)),
        check_vma=False,
    )
```

```python
import functools
import math

import jax
import jax.numpy as jnp
from jax import lax
from jax.experimental import pallas as pl
from jax.experimental.pallas import tpu as pltpu
from jax.sharding import PartitionSpec as P

REACH = 6
DEPTH = 2
AMPLITUDE = 0.02
F32 = jnp.float32
BF16 = jnp.bfloat16
NN = (((1,), (0,)), ((), ()))
NT = (((1,), (1,)), ((), ()))
MESH = pl.DeviceIdType.MESH
GROUP = 8


def halves(x):
    hi = x.astype(BF16)
    lo = (x - hi.astype(F32)).astype(BF16)
    return hi, lo


def dot3(a, bhi, blo, dims):
    n = a.shape[0]
    hi, lo = halves(a)
    both = lax.dot_general(
        jnp.concatenate([hi, lo], axis=0), bhi, dims, preferred_element_type=F32
    )
    rest = lax.dot_general(hi, blo, dims, preferred_element_type=F32)
    return both[:n] + both[n:] + rest


def spread(a, bcat):
    hi, lo = halves(a)
    return lax.dot_general(
        jnp.concatenate([hi, lo], axis=0), bcat, NT, preferred_element_type=F32
    )


def gathered(r):
    n, k = r.shape[0] // 2, r.shape[1] // 2
    return r[:n, :k] + r[n:, :k] + r[:n, k:]


def kernel(
    cycle,
    n_lon,
    n_band,
    pos_ref,
    sky_ref,
    noise_ref,
    basis_ref,
    couple_ref,
    transfer_ref,
    pcouple_ref,
    near_ref,
    far_ref,
    plist_ref,
    home_ref,
    sol_ref,
    res_ref,
    posx,
    posc,
    v0,
    v1,
    w2,
    dirs,
    resid,
    c0,
    c1,
    pc0,
    pc1,
    pf,
    vs,
    khi,
    klo,
    bcat,
    wcat,
    tcat,
    ghi,
    glo,
    red_lon,
    red_band,
    send_sem,
    recv_sem,
):
    maps, leaves, pixels = sky_ref.shape
    rank = basis_ref.shape[1]
    panels = pcouple_ref.shape[0]
    slots = far_ref.shape[0]
    near_slots = near_ref.shape[0]
    lon = lax.axis_index("lon")
    band = lax.axis_index("band")
    right = lax.rem(lon + 1, n_lon)
    left = lax.rem(lon + n_lon - 1, n_lon)
    first = band * cycle + lon * leaves
    used = [0]

    def push(src, dst, target):
        at = used[0]
        used[0] += 1
        copy = pltpu.make_async_remote_copy(
            src_ref=src,
            dst_ref=dst,
            send_sem=send_sem.at[at],
            recv_sem=recv_sem.at[at],
            device_id=target,
            device_id_type=MESH,
        )
        copy.start()
        return copy

    def rim_push(buf, depth):
        return [
            push(buf.at[pl.ds(leaves, depth)], buf.at[pl.ds(0, depth)], {"lon": right}),
            push(
                buf.at[pl.ds(depth, depth)],
                buf.at[pl.ds(depth + leaves, depth)],
                {"lon": left},
            ),
        ]

    def axis_push(buf, axis, me, count):
        return [
            push(buf.at[me], buf.at[me], {axis: lax.rem(me + k, count)}) for k in range(1, count)
        ]

    def landed(copies):
        for copy in copies:
            copy.wait_recv()

    pending = []

    barrier = pltpu.get_barrier_semaphore()
    for k in range(1, n_lon):
        pl.semaphore_signal(
            barrier, inc=1, device_id={"lon": lax.rem(lon + k, n_lon)}, device_id_type=MESH
        )
    for k in range(1, n_band):
        pl.semaphore_signal(
            barrier, inc=1, device_id={"band": lax.rem(band + k, n_band)}, device_id_type=MESH
        )
    posx[pl.ds(DEPTH, leaves)] = jnp.zeros((leaves,) + posx.shape[1:], F32)
    for i in range(leaves):
        v0[DEPTH + i] = sky_ref[:, i, :]
        for component in range(3):
            posx[DEPTH + i, component : component + 1] = pos_ref[component, i : i + 1]
    pl.semaphore_wait(barrier, n_lon - 1 + n_band - 1)
    pos_copies = rim_push(posx, DEPTH)
    v0_copies = rim_push(v0, DEPTH)
    pending += pos_copies + v0_copies

    def prepare(i):
        top, low = pl.ds(0, rank), pl.ds(rank, rank)
        bcat[i, top], bcat[i, low] = halves(basis_ref[i])
        tcat[i, top], tcat[i, low] = halves(transfer_ref[i])
        beside = jnp.concatenate([couple_ref[i, s] for s in range(slots)], axis=1)
        wcat[i, top], wcat[i, low] = halves(beside)

    def upward(g, values, cx, sums):
        ids = [g * GROUP + u for u in range(GROUP)]
        cs = [gathered(spread(values[u], bcat[i])) for u, i in enumerate(ids)]
        ups = [
            dot3(cs[u], tcat[i, pl.ds(0, rank)], tcat[i, pl.ds(rank, rank)], NN)
            for u, i in enumerate(ids)
        ]
        for u, i in enumerate(ids):
            cx[REACH + i] = cs[u]
            sums = [
                sums[k] + ups[u] * jnp.where(home_ref[0, i] == k, 1.0, 0.0).astype(F32)
                for k in range(panels)
            ]
        return sums

    zero_panels = [jnp.zeros((maps, rank), F32) for _ in range(panels)]

    def first_coeffs(g, sums):
        for u in range(GROUP):
            prepare(g * GROUP + u)
        return upward(g, [v0[DEPTH + g * GROUP + u] for u in range(GROUP)], c0, sums)

    sums = lax.fori_loop(0, leaves // GROUP, first_coeffs, zero_panels)
    for k in range(panels):
        pc0[band, k] = sums[k]
    c0_copies = rim_push(c0, REACH)
    pc0_copies = axis_push(pc0, "band", band, n_band)
    pending += c0_copies + pc0_copies
    for k in range(panels):
        for s in range(plist_ref.shape[1]):
            ghi[k, s], glo[k, s] = halves(pcouple_ref[k, s])

    landed(pos_copies + v0_copies)
    log2e = 1.0 / math.log(2.0)
    scale = log2e * math.sqrt(3.0) / (2.0 * math.pi / cycle)

    def columns(j, carry):
        posc[j] = jnp.transpose(posx[j] * scale)
        hi, lo = halves(v0[j])
        vs[j, pl.ds(0, maps)] = hi
        vs[j, pl.ds(maps, maps)] = lo
        return carry

    lax.fori_loop(0, leaves + 2 * DEPTH, columns, 0)

    def near_product(i):
        values = jnp.concatenate([vs[i + d] for d in range(2 * DEPTH + 1)], axis=1)
        both = lax.dot_general(values, khi[i], NN, preferred_element_type=F32)
        rest = lax.dot_general(values[:maps], klo[i], NN, preferred_element_type=F32)
        return both[:maps] + both[maps:] + rest

    chunk = 64

    def first_near(i, carry):
        rows = posx[DEPTH + i] * scale
        me = near_ref[0, i]
        total = noise_ref[pl.ds(i, 1)] * v0[DEPTH + i]
        for d in range(2 * DEPTH + 1):
            offset = d - DEPTH
            if offset == 0:
                weight = jnp.asarray(AMPLITUDE, F32)
            else:
                weight = jnp.asarray(0.0, F32)
                for s in range(1, near_slots):
                    other = near_ref[s, i]
                    gap = other - me
                    hit = (gap == offset) | (gap == offset - cycle) | (gap == offset + cycle)
                    weight = weight + jnp.where((other >= 0) & hit, AMPLITUDE, 0.0).astype(F32)
            slope = weight * math.log(2.0)
            for q in range(0, pixels, chunk):
                squared = None
                for component in range(3):
                    gap = (
                        posc[i + d, pl.ds(q, chunk), component : component + 1]
                        - rows[component : component + 1]
                    )
                    squared = gap * gap if squared is None else squared + gap * gap
                t = squared * lax.rsqrt(jnp.maximum(squared, 1e-30))
                block = (weight + slope * t) * jnp.exp2(-t)
                hi, lo = halves(block)
                khi[i, pl.ds(d * pixels + q, chunk)] = hi
                klo[i, pl.ds(d * pixels + q, chunk)] = lo
            values = vs[i + d]
            at = pl.ds(d * pixels, pixels)
            both = lax.dot_general(values, khi[i, at], NN, preferred_element_type=F32)
            rest = lax.dot_general(values[:maps], klo[i, at], NN, preferred_element_type=F32)
            total = total + (both[:maps] + both[maps:] + rest)
        v1[DEPTH + i] = total
        return carry

    lax.fori_loop(0, leaves, first_near, 0)

    def panel_far(pcx):
        for k in range(panels):
            total = jnp.zeros((maps, rank), F32)
            for s in range(plist_ref.shape[1]):
                other = plist_ref[k, s] // (n_lon * panels)
                total = total + dot3(pcx[other, k], ghi[k, s], glo[k, s], NT)
            pf[k] = total

    def far(i, cx):
        total = spread(pf[home_ref[0, i]], tcat[i])
        parts = []
        for s in range(slots):
            gap = far_ref[s, i] - (first + i)
            gap = jnp.where(gap > REACH, gap - cycle, gap)
            gap = jnp.where(gap < -REACH, gap + cycle, gap)
            row = jnp.clip(i + REACH + gap, 0, leaves + 2 * REACH - 1)
            parts.append(cx[row])
        total = total + spread(jnp.concatenate(parts, axis=1), wcat[i])
        return dot3(
            gathered(total), bcat[i, pl.ds(0, rank)], bcat[i, pl.ds(rank, rank)], NN
        )

    landed(c0_copies + pc0_copies)
    panel_far(pc0)
    zero = jnp.zeros((maps, pixels), F32)

    def first_far(g, carry):
        sums, rr, pw, ww = carry
        fars = [far(g * GROUP + u, c0) for u in range(GROUP)]
        out = [v1[DEPTH + g * GROUP + u] + fars[u] for u in range(GROUP)]
        sums = upward(g, out, c1, sums)
        for u in range(GROUP):
            i = g * GROUP + u
            p, w = v0[DEPTH + i], out[u]
            v1[DEPTH + i] = w
            rr, pw, ww = rr + p * p, pw + p * w, ww + w * w
        return sums, rr, pw, ww

    sums, rr, pw, ww = lax.fori_loop(
        0, leaves // GROUP, first_far, (zero_panels, zero, zero, zero)
    )
    v1_copies = rim_push(v1, DEPTH)
    for k in range(panels):
        pc1[band, k] = sums[k]
    c1_copies = rim_push(c1, REACH)
    pc1_copies = axis_push(pc1, "band", band, n_band)
    pending += v1_copies + c1_copies + pc1_copies

    lane = lax.broadcasted_iota(jnp.int32, (maps, 128), 1)

    def packed(parts):
        out = jnp.zeros((maps, 128), F32)
        for at, part in enumerate(parts):
            out = jnp.where(lane == at, jnp.sum(part, axis=1, keepdims=True), out)
        return out

    def total_of(buf, count):
        out = buf[0]
        for k in range(1, count):
            out = out + buf[k]
        return out

    red_lon[0, lon] = packed([rr, pw, ww])
    lon_copies = axis_push(red_lon.at[0], "lon", lon, n_lon)
    pending += lon_copies

    def split_value(j, carry):
        hi, lo = halves(v1[j])
        vs[j, pl.ds(0, maps)] = hi
        vs[j, pl.ds(maps, maps)] = lo
        return carry

    def second_near(i, carry):
        w2[i] = noise_ref[pl.ds(i, 1)] * v1[DEPTH + i] + near_product(i)
        return carry

    lax.fori_loop(DEPTH, leaves + DEPTH, split_value, 0)

    batch = 2 * DEPTH

    def second_near_batch(g, carry):
        for u in range(batch):
            second_near(DEPTH + batch * g + u, carry)
        return carry

    lax.fori_loop(0, (leaves - 2 * DEPTH) // batch, second_near_batch, 0)
    landed(lon_copies)
    red_band[0, band] = total_of(red_lon.at[0], n_lon)
    band_copies = axis_push(red_band.at[0], "band", band, n_band)
    pending += band_copies
    landed(v1_copies)
    for j in list(range(DEPTH)) + list(range(leaves + DEPTH, leaves + 2 * DEPTH)):
        split_value(j, 0)
    for i in list(range(DEPTH)) + list(range(leaves - DEPTH, leaves)):
        second_near(i, 0)
    landed(c1_copies + pc1_copies)
    panel_far(pc1)

    landed(band_copies)
    first_sums = total_of(red_band.at[0], n_band)
    rr0, pw0, ww0 = first_sums[:, 0:1], first_sums[:, 1:2], first_sums[:, 2:3]
    step0 = rr0 / pw0
    ratio = (rr0 - 2.0 * step0 * pw0 + step0 * step0 * ww0) / rr0

    def second_far(g, carry):
        rr, pw = carry
        fars = [far(g * GROUP + u, c1) for u in range(GROUP)]
        for u in range(GROUP):
            i = g * GROUP + u
            w = w2[i] + fars[u]
            p, image = v0[DEPTH + i], v1[DEPTH + i]
            residual = p - step0 * image
            direction = residual + ratio * p
            image = (image - step0 * w) + ratio * image
            dirs[i] = direction
            resid[i] = residual
            w2[i] = image
            rr, pw = rr + residual * residual, pw + direction * image
        return rr, pw

    rr, pw = lax.fori_loop(0, leaves // GROUP, second_far, (zero, zero))
    red_lon[1, lon] = packed([rr, pw])
    lon_copies = axis_push(red_lon.at[1], "lon", lon, n_lon)
    landed(lon_copies)
    red_band[1, band] = total_of(red_lon.at[1], n_lon)
    band_copies = axis_push(red_band.at[1], "band", band, n_band)
    landed(band_copies)
    pending += lon_copies + band_copies
    second_sums = total_of(red_band.at[1], n_band)
    step1 = second_sums[:, 0:1] / second_sums[:, 1:2]

    for i in range(leaves):
        sol_ref[:, i, :] = step0 * v0[DEPTH + i] + step1 * dirs[i]
        res_ref[:, i, :] = resid[i] - step1 * w2[i]
    for copy in pending:
        copy.wait_send()


def on_device(
    sky_maps,
    noise_var,
    position,
    leaf_basis,
    leaf_couple,
    transfer,
    panel_couple,
    near_list,
    far_list,
    panel_list,
    leaf_panel,
):
    n_lon = lax.axis_size("lon")
    n_band = lax.axis_size("band")
    maps, leaves, pixels = sky_maps.shape
    rank = leaf_basis.shape[2]
    panels = panel_couple.shape[0]
    slots = far_list.shape[1]
    pslots = panel_list.shape[1]
    span = 2 * DEPTH + 1
    count = 4 * 2 + 2 * 2 + 4 * (n_band - 1) + 2 * (n_lon - 1)
    vmem = pl.BlockSpec(memory_space=pltpu.VMEM)
    smem = pl.BlockSpec(memory_space=pltpu.SMEM)
    shape = jax.ShapeDtypeStruct((maps, leaves, pixels), F32)
    sol, res = pl.pallas_call(
        functools.partial(kernel, leaves * n_lon, n_lon, n_band),
        out_shape=(shape, shape),
        in_specs=[vmem] * 7 + [smem] * 4,
        out_specs=(vmem, vmem),
        scratch_shapes=[
            pltpu.VMEM((leaves + 2 * DEPTH, 8, pixels), F32),
            pltpu.VMEM((leaves + 2 * DEPTH, pixels, 8), F32),
            pltpu.VMEM((leaves + 2 * DEPTH, maps, pixels), F32),
            pltpu.VMEM((leaves + 2 * DEPTH, maps, pixels), F32),
            pltpu.VMEM((leaves, maps, pixels), F32),
            pltpu.VMEM((leaves, maps, pixels), F32),
            pltpu.VMEM((leaves, maps, pixels), F32),
            pltpu.VMEM((leaves + 2 * REACH, maps, rank), F32),
            pltpu.VMEM((leaves + 2 * REACH, maps, rank), F32),
            pltpu.VMEM((n_band, panels, maps, rank), F32),
            pltpu.VMEM((n_band, panels, maps, rank), F32),
            pltpu.VMEM((panels, maps, rank), F32),
            pltpu.VMEM((leaves + 2 * DEPTH, 2 * maps, pixels), BF16),
            pltpu.VMEM((leaves, span * pixels, pixels), BF16),
            pltpu.VMEM((leaves, span * pixels, pixels), BF16),
            pltpu.VMEM((leaves, 2 * rank, pixels), BF16),
            pltpu.VMEM((leaves, 2 * rank, slots * rank), BF16),
            pltpu.VMEM((leaves, 2 * rank, rank), BF16),
            pltpu.VMEM((panels, pslots, rank, rank), BF16),
            pltpu.VMEM((panels, pslots, rank, rank), BF16),
            pltpu.VMEM((2, n_lon, maps, 128), F32),
            pltpu.VMEM((2, n_band, maps, 128), F32),
            pltpu.SemaphoreType.DMA((count,)),
            pltpu.SemaphoreType.DMA((count,)),
        ],
        compiler_params=pltpu.CompilerParams(
            collective_id=0, has_side_effects=True, vmem_limit_bytes=56 * 1024 * 1024
        ),
        cost_estimate=pl.CostEstimate(
            flops=4 * leaves * span * pixels * pixels * maps,
            bytes_accessed=8 * 1024 * 1024,
            transcendentals=2 * leaves * span * pixels * pixels,
        ),
    )(
        position,
        sky_maps,
        noise_var,
        jnp.swapaxes(leaf_basis, 1, 2),
        leaf_couple,
        transfer,
        panel_couple,
        near_list.T,
        far_list.T,
        panel_list,
        leaf_panel[None],
    )
    return (sol, res)


def solution(mesh):
    placed = (
        P(None, ("band", "lon"), None),
        P(("band", "lon"), None),
        P(None, ("band", "lon"), None),
        P(("band", "lon"), None, None),
        P(("band", "lon"), None, None, None),
        P(("band", "lon"), None, None),
        P(("band", "lon"), None, None, None),
        P(("band", "lon"), None),
        P(("band", "lon"), None),
        P(("band", "lon"), None),
        P(("band", "lon")),
    )
    return jax.shard_map(
        on_device,
        mesh=mesh,
        in_specs=placed,
        out_specs=(P(None, ("band", "lon"), None), P(None, ("band", "lon"), None)),
        check_vma=False,
    )
```

```python
import functools
import math

import jax
import jax.numpy as jnp
from jax import lax
from jax.experimental import pallas as pl
from jax.experimental.pallas import tpu as pltpu
from jax.sharding import PartitionSpec as P

REACH = 6
DEPTH = 2
AMPLITUDE = 0.02
F32 = jnp.float32
BF16 = jnp.bfloat16
NN = (((1,), (0,)), ((), ()))
NT = (((1,), (1,)), ((), ()))
MESH = pl.DeviceIdType.MESH
GROUP = 8


def halves(x):
    hi = x.astype(BF16)
    lo = (x - hi.astype(F32)).astype(BF16)
    return hi, lo


def dot3(a, bhi, blo, dims):
    n = a.shape[0]
    hi, lo = halves(a)
    both = lax.dot_general(
        jnp.concatenate([hi, lo], axis=0), bhi, dims, preferred_element_type=F32
    )
    rest = lax.dot_general(hi, blo, dims, preferred_element_type=F32)
    return both[:n] + both[n:] + rest


def kernel(
    cycle,
    n_lon,
    n_band,
    pos_ref,
    sky_ref,
    noise_ref,
    basis_ref,
    couple_ref,
    transfer_ref,
    pcouple_ref,
    near_ref,
    far_ref,
    plist_ref,
    home_ref,
    sol_ref,
    res_ref,
    posx,
    posc,
    v0,
    v1,
    w2,
    dirs,
    resid,
    c0,
    c1,
    pc0,
    pc1,
    pf,
    vs,
    khi,
    klo,
    bhi,
    blo,
    whi,
    wlo,
    thi,
    tlo,
    ghi,
    glo,
    red_lon,
    red_band,
    send_sem,
    recv_sem,
):
    maps, leaves, pixels = sky_ref.shape
    rank = basis_ref.shape[1]
    panels = pcouple_ref.shape[0]
    slots = far_ref.shape[0]
    near_slots = near_ref.shape[0]
    lon = lax.axis_index("lon")
    band = lax.axis_index("band")
    right = lax.rem(lon + 1, n_lon)
    left = lax.rem(lon + n_lon - 1, n_lon)
    first = band * cycle + lon * leaves
    used = [0]

    def push(src, dst, target):
        at = used[0]
        used[0] += 1
        copy = pltpu.make_async_remote_copy(
            src_ref=src,
            dst_ref=dst,
            send_sem=send_sem.at[at],
            recv_sem=recv_sem.at[at],
            device_id=target,
            device_id_type=MESH,
        )
        copy.start()
        return copy

    def rim_push(buf, depth):
        return [
            push(buf.at[pl.ds(leaves, depth)], buf.at[pl.ds(0, depth)], {"lon": right}),
            push(
                buf.at[pl.ds(depth, depth)],
                buf.at[pl.ds(depth + leaves, depth)],
                {"lon": left},
            ),
        ]

    def axis_push(buf, axis, me, count):
        return [
            push(buf.at[me], buf.at[me], {axis: lax.rem(me + k, count)}) for k in range(1, count)
        ]

    def landed(copies):
        for copy in copies:
            copy.wait_recv()

    pending = []

    barrier = pltpu.get_barrier_semaphore()
    for k in range(1, n_lon):
        pl.semaphore_signal(
            barrier, inc=1, device_id={"lon": lax.rem(lon + k, n_lon)}, device_id_type=MESH
        )
    for k in range(1, n_band):
        pl.semaphore_signal(
            barrier, inc=1, device_id={"band": lax.rem(band + k, n_band)}, device_id_type=MESH
        )
    posx[pl.ds(DEPTH, leaves)] = jnp.zeros((leaves,) + posx.shape[1:], F32)
    for i in range(leaves):
        v0[DEPTH + i] = sky_ref[:, i, :]
        for component in range(3):
            posx[DEPTH + i, component : component + 1] = pos_ref[component, i : i + 1]
    pl.semaphore_wait(barrier, n_lon - 1 + n_band - 1)
    pos_copies = rim_push(posx, DEPTH)
    v0_copies = rim_push(v0, DEPTH)
    pending += pos_copies + v0_copies

    def prepare(i):
        bhi[i], blo[i] = halves(basis_ref[i])
        thi[i], tlo[i] = halves(transfer_ref[i])
        for s in range(slots):
            whi[i, s], wlo[i, s] = halves(couple_ref[i, s])

    def upward(g, values, cx, sums):
        ids = [g * GROUP + u for u in range(GROUP)]
        cs = [dot3(values[u], bhi[i], blo[i], NT) for u, i in enumerate(ids)]
        ups = [dot3(cs[u], thi[i], tlo[i], NN) for u, i in enumerate(ids)]
        for u, i in enumerate(ids):
            cx[REACH + i] = cs[u]
            sums = [
                sums[k] + ups[u] * jnp.where(home_ref[0, i] == k, 1.0, 0.0).astype(F32)
                for k in range(panels)
            ]
        return sums

    zero_panels = [jnp.zeros((maps, rank), F32) for _ in range(panels)]

    def first_coeffs(g, sums):
        for u in range(GROUP):
            prepare(g * GROUP + u)
        return upward(g, [v0[DEPTH + g * GROUP + u] for u in range(GROUP)], c0, sums)

    sums = lax.fori_loop(0, leaves // GROUP, first_coeffs, zero_panels)
    for k in range(panels):
        pc0[band, k] = sums[k]
    c0_copies = rim_push(c0, REACH)
    pc0_copies = axis_push(pc0, "band", band, n_band)
    pending += c0_copies + pc0_copies
    for k in range(panels):
        for s in range(plist_ref.shape[1]):
            ghi[k, s], glo[k, s] = halves(pcouple_ref[k, s])

    landed(pos_copies + v0_copies)
    log2e = 1.0 / math.log(2.0)
    scale = log2e * math.sqrt(3.0) / (2.0 * math.pi / cycle)

    def columns(j, carry):
        posc[j] = jnp.transpose(posx[j] * scale)
        hi, lo = halves(v0[j])
        vs[j, pl.ds(0, maps)] = hi
        vs[j, pl.ds(maps, maps)] = lo
        return carry

    lax.fori_loop(0, leaves + 2 * DEPTH, columns, 0)

    def near_product(i):
        values = jnp.concatenate([vs[i + d] for d in range(2 * DEPTH + 1)], axis=1)
        both = lax.dot_general(values, khi[i], NN, preferred_element_type=F32)
        rest = lax.dot_general(values[:maps], klo[i], NN, preferred_element_type=F32)
        return both[:maps] + both[maps:] + rest

    chunk = 32

    def first_near(i, carry):
        rows = posx[DEPTH + i] * scale
        me = near_ref[0, i]
        total = noise_ref[pl.ds(i, 1)] * v0[DEPTH + i]
        for d in range(2 * DEPTH + 1):
            offset = d - DEPTH
            if offset == 0:
                weight = jnp.asarray(AMPLITUDE, F32)
            else:
                weight = jnp.asarray(0.0, F32)
                for s in range(1, near_slots):
                    other = near_ref[s, i]
                    gap = other - me
                    hit = (gap == offset) | (gap == offset - cycle) | (gap == offset + cycle)
                    weight = weight + jnp.where((other >= 0) & hit, AMPLITUDE, 0.0).astype(F32)
            slope = weight * math.log(2.0)
            for q in range(0, pixels, chunk):
                squared = None
                for component in range(3):
                    gap = (
                        posc[i + d, pl.ds(q, chunk), component : component + 1]
                        - rows[component : component + 1]
                    )
                    squared = gap * gap if squared is None else squared + gap * gap
                t = squared * lax.rsqrt(jnp.maximum(squared, 1e-30))
                block = (weight + slope * t) * jnp.exp2(-t)
                hi, lo = halves(block)
                khi[i, pl.ds(d * pixels + q, chunk)] = hi
                klo[i, pl.ds(d * pixels + q, chunk)] = lo
            values = vs[i + d]
            at = pl.ds(d * pixels, pixels)
            both = lax.dot_general(values, khi[i, at], NN, preferred_element_type=F32)
            rest = lax.dot_general(values[:maps], klo[i, at], NN, preferred_element_type=F32)
            total = total + (both[:maps] + both[maps:] + rest)
        v1[DEPTH + i] = total
        return carry

    lax.fori_loop(0, leaves, first_near, 0)

    def panel_far(pcx):
        for k in range(panels):
            total = jnp.zeros((maps, rank), F32)
            for s in range(plist_ref.shape[1]):
                other = plist_ref[k, s] // (n_lon * panels)
                total = total + dot3(pcx[other, k], ghi[k, s], glo[k, s], NT)
            pf[k] = total

    def far(i, cx):
        total = dot3(pf[home_ref[0, i]], thi[i], tlo[i], NT)
        for s in range(slots):
            gap = far_ref[s, i] - (first + i)
            gap = jnp.where(gap > REACH, gap - cycle, gap)
            gap = jnp.where(gap < -REACH, gap + cycle, gap)
            row = jnp.clip(i + REACH + gap, 0, leaves + 2 * REACH - 1)
            total = total + dot3(cx[row], whi[i, s], wlo[i, s], NT)
        return dot3(total, bhi[i], blo[i], NN)

    landed(c0_copies + pc0_copies)
    panel_far(pc0)
    zero = jnp.zeros((maps, pixels), F32)

    def first_far(g, carry):
        sums, rr, pw, ww = carry
        fars = [far(g * GROUP + u, c0) for u in range(GROUP)]
        out = [v1[DEPTH + g * GROUP + u] + fars[u] for u in range(GROUP)]
        sums = upward(g, out, c1, sums)
        for u in range(GROUP):
            i = g * GROUP + u
            p, w = v0[DEPTH + i], out[u]
            v1[DEPTH + i] = w
            rr, pw, ww = rr + p * p, pw + p * w, ww + w * w
        return sums, rr, pw, ww

    sums, rr, pw, ww = lax.fori_loop(
        0, leaves // GROUP, first_far, (zero_panels, zero, zero, zero)
    )
    v1_copies = rim_push(v1, DEPTH)
    for k in range(panels):
        pc1[band, k] = sums[k]
    c1_copies = rim_push(c1, REACH)
    pc1_copies = axis_push(pc1, "band", band, n_band)
    pending += v1_copies + c1_copies + pc1_copies

    lane = lax.broadcasted_iota(jnp.int32, (maps, 128), 1)

    def packed(parts):
        out = jnp.zeros((maps, 128), F32)
        for at, part in enumerate(parts):
            out = jnp.where(lane == at, jnp.sum(part, axis=1, keepdims=True), out)
        return out

    def total_of(buf, count):
        out = buf[0]
        for k in range(1, count):
            out = out + buf[k]
        return out

    red_lon[0, lon] = packed([rr, pw, ww])
    lon_copies = axis_push(red_lon.at[0], "lon", lon, n_lon)
    pending += lon_copies

    def split_value(j, carry):
        hi, lo = halves(v1[j])
        vs[j, pl.ds(0, maps)] = hi
        vs[j, pl.ds(maps, maps)] = lo
        return carry

    def second_near(i, carry):
        w2[i] = noise_ref[pl.ds(i, 1)] * v1[DEPTH + i] + near_product(i)
        return carry

    lax.fori_loop(DEPTH, leaves + DEPTH, split_value, 0)

    batch = 2 * DEPTH

    def second_near_batch(g, carry):
        for u in range(batch):
            second_near(DEPTH + batch * g + u, carry)
        return carry

    lax.fori_loop(0, (leaves - 2 * DEPTH) // batch, second_near_batch, 0)
    landed(lon_copies)
    red_band[0, band] = total_of(red_lon.at[0], n_lon)
    band_copies = axis_push(red_band.at[0], "band", band, n_band)
    pending += band_copies
    landed(v1_copies)
    for j in list(range(DEPTH)) + list(range(leaves + DEPTH, leaves + 2 * DEPTH)):
        split_value(j, 0)
    for i in list(range(DEPTH)) + list(range(leaves - DEPTH, leaves)):
        second_near(i, 0)
    landed(c1_copies + pc1_copies)
    panel_far(pc1)

    landed(band_copies)
    first_sums = total_of(red_band.at[0], n_band)
    rr0, pw0, ww0 = first_sums[:, 0:1], first_sums[:, 1:2], first_sums[:, 2:3]
    step0 = rr0 / pw0
    ratio = (rr0 - 2.0 * step0 * pw0 + step0 * step0 * ww0) / rr0

    def second_far(g, carry):
        rr, pw = carry
        fars = [far(g * GROUP + u, c1) for u in range(GROUP)]
        for u in range(GROUP):
            i = g * GROUP + u
            w = w2[i] + fars[u]
            p, image = v0[DEPTH + i], v1[DEPTH + i]
            residual = p - step0 * image
            direction = residual + ratio * p
            image = (image - step0 * w) + ratio * image
            dirs[i] = direction
            resid[i] = residual
            w2[i] = image
            rr, pw = rr + residual * residual, pw + direction * image
        return rr, pw

    rr, pw = lax.fori_loop(0, leaves // GROUP, second_far, (zero, zero))
    red_lon[1, lon] = packed([rr, pw])
    lon_copies = axis_push(red_lon.at[1], "lon", lon, n_lon)
    landed(lon_copies)
    red_band[1, band] = total_of(red_lon.at[1], n_lon)
    band_copies = axis_push(red_band.at[1], "band", band, n_band)
    landed(band_copies)
    pending += lon_copies + band_copies
    second_sums = total_of(red_band.at[1], n_band)
    step1 = second_sums[:, 0:1] / second_sums[:, 1:2]

    for i in range(leaves):
        sol_ref[:, i, :] = step0 * v0[DEPTH + i] + step1 * dirs[i]
        res_ref[:, i, :] = resid[i] - step1 * w2[i]
    for copy in pending:
        copy.wait_send()


def on_device(
    sky_maps,
    noise_var,
    position,
    leaf_basis,
    leaf_couple,
    transfer,
    panel_couple,
    near_list,
    far_list,
    panel_list,
    leaf_panel,
):
    n_lon = lax.axis_size("lon")
    n_band = lax.axis_size("band")
    maps, leaves, pixels = sky_maps.shape
    rank = leaf_basis.shape[2]
    panels = panel_couple.shape[0]
    slots = far_list.shape[1]
    pslots = panel_list.shape[1]
    span = 2 * DEPTH + 1
    count = 4 * 2 + 2 * 2 + 4 * (n_band - 1) + 2 * (n_lon - 1)
    vmem = pl.BlockSpec(memory_space=pltpu.VMEM)
    smem = pl.BlockSpec(memory_space=pltpu.SMEM)
    shape = jax.ShapeDtypeStruct((maps, leaves, pixels), F32)
    sol, res = pl.pallas_call(
        functools.partial(kernel, leaves * n_lon, n_lon, n_band),
        out_shape=(shape, shape),
        in_specs=[vmem] * 7 + [smem] * 4,
        out_specs=(vmem, vmem),
        scratch_shapes=[
            pltpu.VMEM((leaves + 2 * DEPTH, 8, pixels), F32),
            pltpu.VMEM((leaves + 2 * DEPTH, pixels, 8), F32),
            pltpu.VMEM((leaves + 2 * DEPTH, maps, pixels), F32),
            pltpu.VMEM((leaves + 2 * DEPTH, maps, pixels), F32),
            pltpu.VMEM((leaves, maps, pixels), F32),
            pltpu.VMEM((leaves, maps, pixels), F32),
            pltpu.VMEM((leaves, maps, pixels), F32),
            pltpu.VMEM((leaves + 2 * REACH, maps, rank), F32),
            pltpu.VMEM((leaves + 2 * REACH, maps, rank), F32),
            pltpu.VMEM((n_band, panels, maps, rank), F32),
            pltpu.VMEM((n_band, panels, maps, rank), F32),
            pltpu.VMEM((panels, maps, rank), F32),
            pltpu.VMEM((leaves + 2 * DEPTH, 2 * maps, pixels), BF16),
            pltpu.VMEM((leaves, span * pixels, pixels), BF16),
            pltpu.VMEM((leaves, span * pixels, pixels), BF16),
            pltpu.VMEM((leaves, rank, pixels), BF16),
            pltpu.VMEM((leaves, rank, pixels), BF16),
            pltpu.VMEM((leaves, slots, rank, rank), BF16),
            pltpu.VMEM((leaves, slots, rank, rank), BF16),
            pltpu.VMEM((leaves, rank, rank), BF16),
            pltpu.VMEM((leaves, rank, rank), BF16),
            pltpu.VMEM((panels, pslots, rank, rank), BF16),
            pltpu.VMEM((panels, pslots, rank, rank), BF16),
            pltpu.VMEM((2, n_lon, maps, 128), F32),
            pltpu.VMEM((2, n_band, maps, 128), F32),
            pltpu.SemaphoreType.DMA((count,)),
            pltpu.SemaphoreType.DMA((count,)),
        ],
        compiler_params=pltpu.CompilerParams(
            collective_id=0, has_side_effects=True, vmem_limit_bytes=56 * 1024 * 1024
        ),
        cost_estimate=pl.CostEstimate(
            flops=4 * leaves * span * pixels * pixels * maps,
            bytes_accessed=8 * 1024 * 1024,
            transcendentals=2 * leaves * span * pixels * pixels,
        ),
    )(
        position,
        sky_maps,
        noise_var,
        jnp.swapaxes(leaf_basis, 1, 2),
        leaf_couple,
        transfer,
        panel_couple,
        near_list.T,
        far_list.T,
        panel_list,
        leaf_panel[None],
    )
    return (sol, res)


def solution(mesh):
    placed = (
        P(None, ("band", "lon"), None),
        P(("band", "lon"), None),
        P(None, ("band", "lon"), None),
        P(("band", "lon"), None, None),
        P(("band", "lon"), None, None, None),
        P(("band", "lon"), None, None),
        P(("band", "lon"), None, None, None),
        P(("band", "lon"), None),
        P(("band", "lon"), None),
        P(("band", "lon"), None),
        P(("band", "lon")),
    )
    return jax.shard_map(
        on_device,
        mesh=mesh,
        in_specs=placed,
        out_specs=(P(None, ("band", "lon"), None), P(None, ("band", "lon"), None)),
        check_vma=False,
    )
```

```python
import functools
import math

import jax
import jax.numpy as jnp
from jax import lax
from jax.experimental import pallas as pl
from jax.experimental.pallas import tpu as pltpu
from jax.sharding import PartitionSpec as P

REACH = 6
DEPTH = 2
AMPLITUDE = 0.02
F32 = jnp.float32
BF16 = jnp.bfloat16
NN = (((1,), (0,)), ((), ()))
NT = (((1,), (1,)), ((), ()))
MESH = pl.DeviceIdType.MESH
GROUP = 8


def halves(x):
    hi = x.astype(BF16)
    lo = (x - hi.astype(F32)).astype(BF16)
    return hi, lo


def dot3(a, bhi, blo, dims):
    n = a.shape[0]
    hi, lo = halves(a)
    both = lax.dot_general(
        jnp.concatenate([hi, lo], axis=0), bhi, dims, preferred_element_type=F32
    )
    rest = lax.dot_general(hi, blo, dims, preferred_element_type=F32)
    return both[:n] + both[n:] + rest


def kernel(
    cycle,
    n_lon,
    n_band,
    pos_ref,
    sky_ref,
    noise_ref,
    basis_ref,
    couple_ref,
    transfer_ref,
    pcouple_ref,
    near_ref,
    far_ref,
    plist_ref,
    home_ref,
    sol_ref,
    res_ref,
    posx,
    posc,
    v0,
    v1,
    w2,
    dirs,
    resid,
    c0,
    c1,
    pc0,
    pc1,
    pf,
    vs,
    khi,
    klo,
    bhi,
    blo,
    whi,
    wlo,
    thi,
    tlo,
    ghi,
    glo,
    red_lon,
    red_band,
    send_sem,
    recv_sem,
):
    maps, leaves, pixels = sky_ref.shape
    rank = basis_ref.shape[1]
    panels = pcouple_ref.shape[0]
    slots = far_ref.shape[0]
    near_slots = near_ref.shape[0]
    lon = lax.axis_index("lon")
    band = lax.axis_index("band")
    right = lax.rem(lon + 1, n_lon)
    left = lax.rem(lon + n_lon - 1, n_lon)
    first = band * cycle + lon * leaves
    used = [0]

    def push(src, dst, target):
        at = used[0]
        used[0] += 1
        copy = pltpu.make_async_remote_copy(
            src_ref=src,
            dst_ref=dst,
            send_sem=send_sem.at[at],
            recv_sem=recv_sem.at[at],
            device_id=target,
            device_id_type=MESH,
        )
        copy.start()
        return copy

    def rim_push(buf, depth):
        return [
            push(buf.at[pl.ds(leaves, depth)], buf.at[pl.ds(0, depth)], {"lon": right}),
            push(
                buf.at[pl.ds(depth, depth)],
                buf.at[pl.ds(depth + leaves, depth)],
                {"lon": left},
            ),
        ]

    def axis_push(buf, axis, me, count):
        return [
            push(buf.at[me], buf.at[me], {axis: lax.rem(me + k, count)}) for k in range(1, count)
        ]

    def landed(copies):
        for copy in copies:
            copy.wait_recv()

    pending = []

    barrier = pltpu.get_barrier_semaphore()
    for k in range(1, n_lon):
        pl.semaphore_signal(
            barrier, inc=1, device_id={"lon": lax.rem(lon + k, n_lon)}, device_id_type=MESH
        )
    for k in range(1, n_band):
        pl.semaphore_signal(
            barrier, inc=1, device_id={"band": lax.rem(band + k, n_band)}, device_id_type=MESH
        )
    posx[pl.ds(DEPTH, leaves)] = jnp.zeros((leaves,) + posx.shape[1:], F32)
    for i in range(leaves):
        v0[DEPTH + i] = sky_ref[:, i, :]
        for component in range(3):
            posx[DEPTH + i, component : component + 1] = pos_ref[component, i : i + 1]
    pl.semaphore_wait(barrier, n_lon - 1 + n_band - 1)
    pos_copies = rim_push(posx, DEPTH)
    v0_copies = rim_push(v0, DEPTH)
    pending += pos_copies + v0_copies

    def prepare(i):
        bhi[i], blo[i] = halves(basis_ref[i])
        thi[i], tlo[i] = halves(transfer_ref[i])
        for s in range(slots):
            whi[i, s], wlo[i, s] = halves(couple_ref[i, s])

    def upward(g, values, cx, sums):
        ids = [g * GROUP + u for u in range(GROUP)]
        cs = [dot3(values[u], bhi[i], blo[i], NT) for u, i in enumerate(ids)]
        ups = [dot3(cs[u], thi[i], tlo[i], NN) for u, i in enumerate(ids)]
        for u, i in enumerate(ids):
            cx[REACH + i] = cs[u]
            sums = [
                sums[k] + ups[u] * jnp.where(home_ref[0, i] == k, 1.0, 0.0).astype(F32)
                for k in range(panels)
            ]
        return sums

    zero_panels = [jnp.zeros((maps, rank), F32) for _ in range(panels)]

    def first_coeffs(g, sums):
        for u in range(GROUP):
            prepare(g * GROUP + u)
        return upward(g, [v0[DEPTH + g * GROUP + u] for u in range(GROUP)], c0, sums)

    sums = lax.fori_loop(0, leaves // GROUP, first_coeffs, zero_panels)
    for k in range(panels):
        pc0[band, k] = sums[k]
    c0_copies = rim_push(c0, REACH)
    pc0_copies = axis_push(pc0, "band", band, n_band)
    pending += c0_copies + pc0_copies
    for k in range(panels):
        for s in range(plist_ref.shape[1]):
            ghi[k, s], glo[k, s] = halves(pcouple_ref[k, s])

    landed(pos_copies + v0_copies)
    log2e = 1.0 / math.log(2.0)
    scale = log2e * math.sqrt(3.0) / (2.0 * math.pi / cycle)

    def columns(j, carry):
        turned = jnp.transpose(posx[j] * scale)
        for component in range(3):
            posc[j, component] = jnp.broadcast_to(
                turned[:, component : component + 1], (pixels, 128)
            )
        hi, lo = halves(v0[j])
        vs[j, pl.ds(0, maps)] = hi
        vs[j, pl.ds(maps, maps)] = lo
        return carry

    lax.fori_loop(0, leaves + 2 * DEPTH, columns, 0)

    def near_product(i):
        values = jnp.concatenate([vs[i + d] for d in range(2 * DEPTH + 1)], axis=1)
        both = lax.dot_general(values, khi[i], NN, preferred_element_type=F32)
        rest = lax.dot_general(values[:maps], klo[i], NN, preferred_element_type=F32)
        return both[:maps] + both[maps:] + rest

    chunk = 32

    def first_near(i, carry):
        rows = posx[DEPTH + i] * scale
        me = near_ref[0, i]
        total = noise_ref[pl.ds(i, 1)] * v0[DEPTH + i]
        for d in range(2 * DEPTH + 1):
            offset = d - DEPTH
            if offset == 0:
                weight = jnp.asarray(AMPLITUDE, F32)
            else:
                weight = jnp.asarray(0.0, F32)
                for s in range(1, near_slots):
                    other = near_ref[s, i]
                    gap = other - me
                    hit = (gap == offset) | (gap == offset - cycle) | (gap == offset + cycle)
                    weight = weight + jnp.where((other >= 0) & hit, AMPLITUDE, 0.0).astype(F32)
            slope = weight * math.log(2.0)
            for q in range(0, pixels, chunk):
                for p in range(0, pixels, 128):
                    squared = None
                    for component in range(3):
                        gap = (
                            posc[i + d, component, pl.ds(q, chunk)]
                            - rows[component : component + 1, p : p + 128]
                        )
                        squared = gap * gap if squared is None else squared + gap * gap
                    t = squared * lax.rsqrt(jnp.maximum(squared, 1e-30))
                    block = (weight + slope * t) * jnp.exp2(-t)
                    hi, lo = halves(block)
                    khi[i, pl.ds(d * pixels + q, chunk), pl.ds(p, 128)] = hi
                    klo[i, pl.ds(d * pixels + q, chunk), pl.ds(p, 128)] = lo
            values = vs[i + d]
            at = pl.ds(d * pixels, pixels)
            both = lax.dot_general(values, khi[i, at], NN, preferred_element_type=F32)
            rest = lax.dot_general(values[:maps], klo[i, at], NN, preferred_element_type=F32)
            total = total + (both[:maps] + both[maps:] + rest)
        v1[DEPTH + i] = total
        return carry

    lax.fori_loop(0, leaves, first_near, 0)

    def panel_far(pcx):
        for k in range(panels):
            total = jnp.zeros((maps, rank), F32)
            for s in range(plist_ref.shape[1]):
                other = plist_ref[k, s] // (n_lon * panels)
                total = total + dot3(pcx[other, k], ghi[k, s], glo[k, s], NT)
            pf[k] = total

    def far(i, cx):
        total = dot3(pf[home_ref[0, i]], thi[i], tlo[i], NT)
        for s in range(slots):
            gap = far_ref[s, i] - (first + i)
            gap = jnp.where(gap > REACH, gap - cycle, gap)
            gap = jnp.where(gap < -REACH, gap + cycle, gap)
            row = jnp.clip(i + REACH + gap, 0, leaves + 2 * REACH - 1)
            total = total + dot3(cx[row], whi[i, s], wlo[i, s], NT)
        return dot3(total, bhi[i], blo[i], NN)

    landed(c0_copies + pc0_copies)
    panel_far(pc0)
    zero = jnp.zeros((maps, pixels), F32)

    def first_far(g, carry):
        sums, rr, pw, ww = carry
        fars = [far(g * GROUP + u, c0) for u in range(GROUP)]
        out = [v1[DEPTH + g * GROUP + u] + fars[u] for u in range(GROUP)]
        sums = upward(g, out, c1, sums)
        for u in range(GROUP):
            i = g * GROUP + u
            p, w = v0[DEPTH + i], out[u]
            v1[DEPTH + i] = w
            rr, pw, ww = rr + p * p, pw + p * w, ww + w * w
        return sums, rr, pw, ww

    sums, rr, pw, ww = lax.fori_loop(
        0, leaves // GROUP, first_far, (zero_panels, zero, zero, zero)
    )
    v1_copies = rim_push(v1, DEPTH)
    for k in range(panels):
        pc1[band, k] = sums[k]
    c1_copies = rim_push(c1, REACH)
    pc1_copies = axis_push(pc1, "band", band, n_band)
    pending += v1_copies + c1_copies + pc1_copies

    lane = lax.broadcasted_iota(jnp.int32, (maps, 128), 1)

    def packed(parts):
        out = jnp.zeros((maps, 128), F32)
        for at, part in enumerate(parts):
            out = jnp.where(lane == at, jnp.sum(part, axis=1, keepdims=True), out)
        return out

    def total_of(buf, count):
        out = buf[0]
        for k in range(1, count):
            out = out + buf[k]
        return out

    red_lon[0, lon] = packed([rr, pw, ww])
    lon_copies = axis_push(red_lon.at[0], "lon", lon, n_lon)
    pending += lon_copies

    def split_value(j, carry):
        hi, lo = halves(v1[j])
        vs[j, pl.ds(0, maps)] = hi
        vs[j, pl.ds(maps, maps)] = lo
        return carry

    def second_near(i, carry):
        w2[i] = noise_ref[pl.ds(i, 1)] * v1[DEPTH + i] + near_product(i)
        return carry

    lax.fori_loop(DEPTH, leaves + DEPTH, split_value, 0)

    batch = 2 * DEPTH

    def second_near_batch(g, carry):
        for u in range(batch):
            second_near(DEPTH + batch * g + u, carry)
        return carry

    lax.fori_loop(0, (leaves - 2 * DEPTH) // batch, second_near_batch, 0)
    landed(lon_copies)
    red_band[0, band] = total_of(red_lon.at[0], n_lon)
    band_copies = axis_push(red_band.at[0], "band", band, n_band)
    pending += band_copies
    landed(v1_copies)
    for j in list(range(DEPTH)) + list(range(leaves + DEPTH, leaves + 2 * DEPTH)):
        split_value(j, 0)
    for i in list(range(DEPTH)) + list(range(leaves - DEPTH, leaves)):
        second_near(i, 0)
    landed(c1_copies + pc1_copies)
    panel_far(pc1)

    landed(band_copies)
    first_sums = total_of(red_band.at[0], n_band)
    rr0, pw0, ww0 = first_sums[:, 0:1], first_sums[:, 1:2], first_sums[:, 2:3]
    step0 = rr0 / pw0
    ratio = (rr0 - 2.0 * step0 * pw0 + step0 * step0 * ww0) / rr0

    def second_far(g, carry):
        rr, pw = carry
        fars = [far(g * GROUP + u, c1) for u in range(GROUP)]
        for u in range(GROUP):
            i = g * GROUP + u
            w = w2[i] + fars[u]
            p, image = v0[DEPTH + i], v1[DEPTH + i]
            residual = p - step0 * image
            direction = residual + ratio * p
            image = (image - step0 * w) + ratio * image
            dirs[i] = direction
            resid[i] = residual
            w2[i] = image
            rr, pw = rr + residual * residual, pw + direction * image
        return rr, pw

    rr, pw = lax.fori_loop(0, leaves // GROUP, second_far, (zero, zero))
    red_lon[1, lon] = packed([rr, pw])
    lon_copies = axis_push(red_lon.at[1], "lon", lon, n_lon)
    landed(lon_copies)
    red_band[1, band] = total_of(red_lon.at[1], n_lon)
    band_copies = axis_push(red_band.at[1], "band", band, n_band)
    landed(band_copies)
    pending += lon_copies + band_copies
    second_sums = total_of(red_band.at[1], n_band)
    step1 = second_sums[:, 0:1] / second_sums[:, 1:2]

    for i in range(leaves):
        sol_ref[:, i, :] = step0 * v0[DEPTH + i] + step1 * dirs[i]
        res_ref[:, i, :] = resid[i] - step1 * w2[i]
    for copy in pending:
        copy.wait_send()


def on_device(
    sky_maps,
    noise_var,
    position,
    leaf_basis,
    leaf_couple,
    transfer,
    panel_couple,
    near_list,
    far_list,
    panel_list,
    leaf_panel,
):
    n_lon = lax.axis_size("lon")
    n_band = lax.axis_size("band")
    maps, leaves, pixels = sky_maps.shape
    rank = leaf_basis.shape[2]
    panels = panel_couple.shape[0]
    slots = far_list.shape[1]
    pslots = panel_list.shape[1]
    span = 2 * DEPTH + 1
    count = 4 * 2 + 2 * 2 + 4 * (n_band - 1) + 2 * (n_lon - 1)
    vmem = pl.BlockSpec(memory_space=pltpu.VMEM)
    smem = pl.BlockSpec(memory_space=pltpu.SMEM)
    shape = jax.ShapeDtypeStruct((maps, leaves, pixels), F32)
    sol, res = pl.pallas_call(
        functools.partial(kernel, leaves * n_lon, n_lon, n_band),
        out_shape=(shape, shape),
        in_specs=[vmem] * 7 + [smem] * 4,
        out_specs=(vmem, vmem),
        scratch_shapes=[
            pltpu.VMEM((leaves + 2 * DEPTH, 8, pixels), F32),
            pltpu.VMEM((leaves + 2 * DEPTH, 3, pixels, 128), F32),
            pltpu.VMEM((leaves + 2 * DEPTH, maps, pixels), F32),
            pltpu.VMEM((leaves + 2 * DEPTH, maps, pixels), F32),
            pltpu.VMEM((leaves, maps, pixels), F32),
            pltpu.VMEM((leaves, maps, pixels), F32),
            pltpu.VMEM((leaves, maps, pixels), F32),
            pltpu.VMEM((leaves + 2 * REACH, maps, rank), F32),
            pltpu.VMEM((leaves + 2 * REACH, maps, rank), F32),
            pltpu.VMEM((n_band, panels, maps, rank), F32),
            pltpu.VMEM((n_band, panels, maps, rank), F32),
            pltpu.VMEM((panels, maps, rank), F32),
            pltpu.VMEM((leaves + 2 * DEPTH, 2 * maps, pixels), BF16),
            pltpu.VMEM((leaves, span * pixels, pixels), BF16),
            pltpu.VMEM((leaves, span * pixels, pixels), BF16),
            pltpu.VMEM((leaves, rank, pixels), BF16),
            pltpu.VMEM((leaves, rank, pixels), BF16),
            pltpu.VMEM((leaves, slots, rank, rank), BF16),
            pltpu.VMEM((leaves, slots, rank, rank), BF16),
            pltpu.VMEM((leaves, rank, rank), BF16),
            pltpu.VMEM((leaves, rank, rank), BF16),
            pltpu.VMEM((panels, pslots, rank, rank), BF16),
            pltpu.VMEM((panels, pslots, rank, rank), BF16),
            pltpu.VMEM((2, n_lon, maps, 128), F32),
            pltpu.VMEM((2, n_band, maps, 128), F32),
            pltpu.SemaphoreType.DMA((count,)),
            pltpu.SemaphoreType.DMA((count,)),
        ],
        compiler_params=pltpu.CompilerParams(
            collective_id=0, has_side_effects=True, vmem_limit_bytes=56 * 1024 * 1024
        ),
        cost_estimate=pl.CostEstimate(
            flops=4 * leaves * span * pixels * pixels * maps,
            bytes_accessed=8 * 1024 * 1024,
            transcendentals=2 * leaves * span * pixels * pixels,
        ),
    )(
        position,
        sky_maps,
        noise_var,
        jnp.swapaxes(leaf_basis, 1, 2),
        leaf_couple,
        transfer,
        panel_couple,
        near_list.T,
        far_list.T,
        panel_list,
        leaf_panel[None],
    )
    return (sol, res)


def solution(mesh):
    placed = (
        P(None, ("band", "lon"), None),
        P(("band", "lon"), None),
        P(None, ("band", "lon"), None),
        P(("band", "lon"), None, None),
        P(("band", "lon"), None, None, None),
        P(("band", "lon"), None, None),
        P(("band", "lon"), None, None, None),
        P(("band", "lon"), None),
        P(("band", "lon"), None),
        P(("band", "lon"), None),
        P(("band", "lon")),
    )
    return jax.shard_map(
        on_device,
        mesh=mesh,
        in_specs=placed,
        out_specs=(P(None, ("band", "lon"), None), P(None, ("band", "lon"), None)),
        check_vma=False,
    )
```
